32 devices in a mesh: outer: 4 (over z), inner: 8 (over y, x, core).
Axes of the slice: x: 2, y: 2, z: 4, core: 2. Of those that a mesh axis runs over, the one named last changes fastest.
Arguments:
- observed: float32 [32768, 768], P(('outer', 'inner')), may hold values from -6 to 6
- leaf_order: int32 [32, 1024], P(('outer', 'inner')), may hold values from 0 to 1023, each once within a row
- leaf_inverse: bfloat16 [32768, 1024], P(('outer', 'inner')), may hold values from -0.1875 to 0.1875
- project_basis: bfloat16 [32768, 640], P(('outer', 'inner')), may hold values from -0.1875 to 0.1875
- correct_basis: bfloat16 [32768, 640], P(('outer', 'inner')), may hold values from -0.375 to 0.375
- coupling: bfloat16 [8192, 256], P(('outer', 'inner'))
- trend_basis: bfloat16 [32768, 256], P(('outer', 'inner')), may hold values from -0.1875 to 0.1875
- trend_correct: bfloat16 [32768, 256], P(('outer', 'inner')), may hold values from -0.375 to 0.375
Outputs:
- solution: float32 [32768, 768], P(('outer', 'inner'))
The draws below stay inside these ranges and needn't reach their ends.
All inputs are finite; a program needn't handle non-finite values.
Results may differ from the reference program's by a relative error of at most 0.013.
Values may be sent and summed in bfloat16 or wider, within the bound.
A program may use at most 64 MiB of HBM per device.

```python
import math
import jax
import jax.numpy as jnp
from jax import lax

LEAF = 1024
RANK = 128
COLS = 768
LEVELS = 5
NPTS = 32768
DEVICES = 32


def draw_coupling(key, part):
    total_rows = DEVICES * 2 * RANK
    row_ids = jnp.arange(total_rows, dtype=jnp.int32)
    slot_ids = row_ids // (2 * RANK)
    lowest = jnp.where(slot_ids == 0, DEVICES, jnp.bitwise_and(slot_ids, -slot_ids))
    scales = 1.0 / jnp.sqrt(lowest.astype(jnp.float32))
    noise = jax.random.normal(key, (total_rows, 2 * RANK), jnp.float32)
    within = row_ids % (2 * RANK)
    column_ids = jnp.arange(2 * RANK, dtype=jnp.int32)
    identity = (within[:, None] == column_ids[None, :]).astype(jnp.float32)
    matrix = (0.5 * identity + 0.5 / math.sqrt(2 * RANK) * noise) * scales[:, None]
    return matrix.astype(jnp.bfloat16)


def block_levels(own_key, shape, split, low, largest):
    factor_of, own = 1.0, jax.random.fold_in(own_key, 6)
    for dim, blocks in split:
        heights = jnp.exp(jax.random.uniform(jax.random.fold_in(own, dim), (blocks,), jnp.float32, low / len(split), largest / len(split)))
        factor_of = factor_of * jnp.repeat(heights, shape[dim] // blocks).reshape([-1 if axis == dim else 1 for axis in range(len(shape))])
    return factor_of


def centred(key, dims, deviation, bound, split=(), kind=jnp.bfloat16):
    level = block_levels(key, dims, split, -0.22, 0.18) if split else 1.0
    drawn = jax.random.normal(key, dims, jnp.float32) * deviation * level
    return jnp.minimum(jnp.maximum(drawn, -bound), bound).astype(kind)


def setup_inputs(seed: int = 0) -> dict:
    key_of = jax.random.split(jax.random.key(seed), 9)
    observed = centred(key_of[0], (NPTS, COLS), 1.0, 6.0, ((0, 32),), jnp.float32)
    leaf_order = jax.vmap(lambda own: jax.random.permutation(own, LEAF))(jax.random.split(key_of[1], DEVICES)).reshape((DEVICES, LEAF)).astype(jnp.int32)
    leaf_inverse = centred(key_of[2], (NPTS, LEAF), LEAF ** -0.5, 0.1875, ((0, 32),))
    project_basis = centred(key_of[3], (NPTS, LEVELS * RANK), LEAF ** -0.5, 0.1875, ((0, 32),))
    correct_basis = centred(key_of[4], (NPTS, LEVELS * RANK), (2 * RANK) ** -0.5, 0.375, ((0, 32),))
    coupling = draw_coupling(jax.random.fold_in(key_of[8], 71), 0)
    trend_basis = centred(key_of[6], (NPTS, 2 * RANK), LEAF ** -0.5, 0.1875, ((0, 32),))
    trend_correct = centred(key_of[7], (NPTS, 2 * RANK), (2 * RANK) ** -0.5, 0.375, ((0, 32),))
    return dict(observed=observed, leaf_order=leaf_order, leaf_inverse=leaf_inverse, project_basis=project_basis, correct_basis=correct_basis, coupling=coupling, trend_basis=trend_basis, trend_correct=trend_correct)


def rounded(values):
    return lax.optimization_barrier(values.astype(jnp.bfloat16)).astype(jnp.float32)


def reference(observed, leaf_order, leaf_inverse, project_basis, correct_basis, coupling, trend_basis, trend_correct):
    leaves = DEVICES
    blocks = observed.reshape(leaves, LEAF, COLS)
    ordered = jax.vmap(lambda block, index: block[index])(blocks, leaf_order)
    inverse = leaf_inverse.reshape(leaves, LEAF, LEAF).astype(jnp.float32)
    estimate = jnp.einsum("nij,njc->nic", inverse, rounded(ordered))
    project_all = project_basis.reshape(leaves, LEAF, LEVELS * RANK)
    correct_all = correct_basis.reshape(leaves, LEAF, LEVELS * RANK)
    blocks_all = coupling.reshape(leaves, 2 * RANK, 2 * RANK)
    for level_no in range(1, LEVELS + 1):
        child = 2 ** (level_no - 1)
        nodes = leaves // (2 * child)
        estimate_bf = rounded(estimate)
        basis = project_all[:, :, (level_no - 1) * RANK:level_no * RANK].astype(jnp.float32)
        projection = jnp.einsum("nkr,nkc->nrc", basis, estimate_bf)
        child_sum = projection.reshape(nodes * 2, child, RANK, COLS).sum(axis=1)
        stacked = child_sum.reshape(nodes, 2 * RANK, COLS)
        owners = (jnp.arange(nodes, dtype=jnp.int32) * (2 * child) + child).astype(jnp.int32)
        matrices = blocks_all[owners].astype(jnp.float32)
        factor = rounded(jnp.einsum("nij,njc->nic", matrices, stacked, precision=lax.Precision.HIGHEST))
        halves = jnp.repeat(factor.reshape(nodes * 2, RANK, COLS), child, axis=0)
        columns = correct_all[:, :, (level_no - 1) * RANK:level_no * RANK].astype(jnp.float32)
        estimate = estimate - jnp.einsum("nkr,nrc->nkc", columns, halves)
    trend_in = trend_basis.reshape(leaves, LEAF, 2 * RANK).astype(jnp.float32)
    trend_sum = jnp.einsum("nkr,nkc->rc", trend_in, rounded(estimate))
    trend_factor = rounded(jnp.dot(blocks_all[0].astype(jnp.float32), rounded(trend_sum)))
    trend_out = trend_correct.reshape(leaves, LEAF, 2 * RANK).astype(jnp.float32)
    solution = estimate - jnp.einsum("nkr,rc->nkc", trend_out, trend_factor)
    return solution.reshape(NPTS, COLS)
```

```python
import functools

import jax
import jax.numpy as jnp
from jax import lax
from jax.experimental import pallas as pl
from jax.experimental.pallas import tpu as pltpu
from jax.sharding import PartitionSpec as P

MESH = pl.DeviceIdType.MESH
BF = jnp.bfloat16
F32 = jnp.float32
NT = (((1,), (1,)), ((), ()))


def dot(a, b):
    return jnp.dot(a, b, preferred_element_type=F32)


def dot_nt(a, b):
    return lax.dot_general(a, b, NT, preferred_element_type=F32)


def plan(cols, levels, rank, trend):
    held, part = [], []
    now = cols
    for _ in range(levels):
        held.append(now)
        if now % 32 == 0:
            now //= 2
        part.append(now)
    rows = [(levels - s) * rank + trend for s in range(levels + 1)]
    width = [sum(rows[s + 1 :]) for s in range(levels)]
    return held, part, rows, width


def sweep_kernel(
    bits_inner,
    levels,
    rank,
    tile,
    observed,
    order,
    inverse,
    project,
    correct,
    coupling,
    trend,
    estimate_out,
    factor_out,
    obs_v,
    obs_bf,
    order_v,
    inv_v,
    basis_v,
    correct_v,
    hot_v,
    est_v,
    est_t,
    blocks,
    factors,
    *rest,
):
    leaf, cols = observed.shape
    trend_rank = trend.shape[1]
    held, part, rows, width = plan(cols, levels, rank, trend_rank)
    sums = rest[: levels + 1]
    x_send = rest[levels + 1 : 2 * levels + 1]
    x_recv = rest[2 * levels + 1 : 3 * levels + 1]
    g_send = rest[3 * levels + 1 : 4 * levels + 1]
    g_recv = rest[4 * levels + 1 : 5 * levels + 1]
    sib = rest[5 * levels + 1 : 6 * levels + 1]
    local_sem, send_sem, recv_sem = rest[6 * levels + 1 :]

    outer, inner = lax.axis_index("outer"), lax.axis_index("inner")
    bits, partners = [], []
    for s in range(levels):
        if s < bits_inner:
            span = 1 << s
            bit = lax.rem(inner // span, 2)
            partners.append((outer, inner + (1 - 2 * bit) * span))
        else:
            span = 1 << (s - bits_inner)
            bit = lax.rem(outer // span, 2)
            partners.append((outer + (1 - 2 * bit) * span, inner))
        bits.append(bit)

    def local(src, dst, i):
        copy = pltpu.make_async_copy(src, dst, local_sem.at[i])
        copy.start()
        return copy

    wide = levels * rank
    c_block = local(coupling, blocks.at[0], 0)
    c_correct = local(correct, correct_v, 1)
    c_project = local(project, basis_v.at[:, pl.ds(0, wide)], 2)
    c_trend = local(trend, basis_v.at[:, pl.ds(wide, trend_rank)], 3)
    c_order = local(order, order_v, 4)
    c_inv = local(inverse, inv_v, 5)
    c_obs = local(observed, obs_v, 6)

    barrier = pltpu.get_barrier_semaphore()
    for partner in partners:
        pl.semaphore_signal(barrier, inc=1, device_id=partner, device_id_type=MESH)
    pl.semaphore_wait(barrier, levels)

    def remote(src, dst, kind, s):
        copy = pltpu.make_async_remote_copy(
            src_ref=src,
            dst_ref=dst,
            send_sem=send_sem.at[kind, s],
            recv_sem=recv_sem.at[kind, s],
            device_id=partners[s],
            device_id_type=MESH,
        )
        copy.start()
        return copy

    flying = []
    block_copies, gram_copies, x_copies, sib_copies = {}, {}, {}, {}
    pending = jnp.int32(0)
    block_of = []

    def send_block(s):
        block_copies[s] = remote(blocks.at[pending], blocks.at[s + 1], 0, s)

    def send_gram(s):
        gram_copies[s] = remote(g_send[s], g_recv[s], 1, s)

    def send_x(s):
        x_copies[s] = remote(x_send[s], x_recv[s], 2, s)

    def finish_small(s):
        nonlocal pending
        block_copies[s].wait_recv()
        block_of.append(jnp.where(bits[s] == 1, pending, s + 1))
        pending = jnp.where(bits[s] == 1, s + 1, pending)
        if s + 1 < levels:
            send_block(s + 1)
        gram_copies[s].wait_recv()
        if s + 1 < levels:
            skip = rows[s + 1]
            g_send[s + 1][...] = (
                g_send[s][:, skip:].astype(F32) + g_recv[s][:, skip:].astype(F32)
            ).astype(BF)
            send_gram(s + 1)

    c_block.wait()
    send_block(0)

    c_correct.wait()
    c_project.wait()
    c_trend.wait()
    at = 0
    for s in range(levels):
        columns_t = correct_v[:, s * rank : (s + 1) * rank].T
        g_send[0][:, at : at + rows[s + 1]] = dot(
            columns_t, basis_v[:, (s + 1) * rank :]
        ).astype(BF)
        at += rows[s + 1]
    send_gram(0)

    c_order.wait()
    steps = leaf // tile

    def make_hot(t, carry):
        r0 = pl.multiple_of(t * tile, tile)
        ids = lax.broadcasted_iota(jnp.int32, (tile, leaf), 0) + r0
        hot_v[pl.ds(r0, tile), :] = jnp.where(ids == order_v[...], 1.0, 0.0).astype(BF)
        return carry

    lax.fori_loop(0, steps, make_hot, 0)
    c_obs.wait()

    def cast(t, carry):
        r0 = pl.multiple_of(t * tile, tile)
        obs_bf[pl.ds(r0, tile), :] = obs_v[pl.ds(r0, tile), :].astype(BF)
        return carry

    lax.fori_loop(0, steps, cast, 0)
    c_inv.wait()

    def make_estimate(t, carry):
        r0 = pl.multiple_of(t * tile, tile)
        ordered_inv = dot_nt(inv_v[pl.ds(r0, tile), :], hot_v[...]).astype(BF)
        value = dot(ordered_inv, obs_bf[...])
        est_v[pl.ds(r0, tile), :] = value
        est_t[:, pl.ds(r0, tile)] = value.astype(BF).T
        return carry

    lax.fori_loop(0, steps, make_estimate, 0)
    c_est = local(est_v, estimate_out, 7)

    finish_small(0)

    half = part[0]
    ctile = half // 2

    def project_half(start, into_send):
        def step(t, carry):
            c0 = pl.multiple_of(start + t * ctile, ctile)
            value = dot(est_t[pl.ds(c0, ctile), :], basis_v[...])
            d0 = pl.multiple_of(t * ctile, ctile)
            if into_send:
                x_send[0][pl.ds(d0, ctile), :] = value.astype(BF)
            else:
                sums[0][pl.ds(d0, ctile), :] = value
            return carry

        lax.fori_loop(0, 2, step, 0)

    project_half((1 - bits[0]) * half, True)
    send_x(0)
    project_half(bits[0] * half, False)

    offsets = [jnp.int32(0)]
    for s in range(levels):
        count = part[s]
        halves = held[s] != part[s]
        first_side = bits[s] == 0
        offset = offsets[s] + (bits[s] * count if halves else 0)
        offset = pl.multiple_of(offset, count)
        offsets.append(offset)
        if s > 0:
            finish_small(s)
        if s == 0 or not halves:
            own = sums[s][...]
        else:
            own = sums[s][pl.ds(pl.multiple_of(bits[s] * count, count), count), :]
        x_copies[s].wait_recv()
        other = x_recv[s][...]
        own_head = own[:, :rank].astype(BF)
        other_head = other[:, :rank]
        one = jnp.where(first_side, own_head.astype(F32), other_head.astype(F32)).astype(BF)
        two = jnp.where(first_side, other_head.astype(F32), own_head.astype(F32)).astype(BF)
        block = blocks[block_of[s]]
        factor = dot_nt(one, block[:, :rank]) + dot_nt(two, block[:, rank:])
        mine = jnp.where(first_side, factor[:, :rank], factor[:, rank:]).astype(BF)
        theirs = jnp.where(first_side, factor[:, rank:], factor[:, :rank]).astype(BF)
        factors[pl.ds(offset, count), s * rank : (s + 1) * rank] = mine
        skip = rows[s + 1]
        new = (
            own[:, rank:]
            + other[:, rank:].astype(F32)
            - dot(mine, g_send[s][:, :skip])
            - dot(theirs, g_recv[s][:, :skip])
        )
        sums[s + 1][...] = new
        if s + 1 < levels:
            after = part[s + 1]
            if held[s + 1] != after:
                away = pl.multiple_of((1 - bits[s + 1]) * after, after)
                x_send[s + 1][...] = sums[s + 1][pl.ds(away, after), :].astype(BF)
            else:
                x_send[s + 1][...] = new.astype(BF)
            send_x(s + 1)
        if halves:
            sib[s][...] = theirs
            sib_copies[s] = remote(
                sib[s],
                factors.at[pl.ds(offset, count), pl.ds(s * rank, rank)],
                3,
                s,
            )

    trend_factor = dot_nt(sums[levels][...].astype(BF), blocks[pending]).astype(BF)
    factors[pl.ds(offsets[levels], part[levels - 1]), wide:] = trend_factor

    down = []
    for s in reversed(range(levels)):
        if s not in sib_copies:
            continue
        lanes = pl.ds((s + 1) * rank, rows[s + 1])
        place = factors.at[pl.ds(offsets[s + 1], part[s]), lanes]
        copy = remote(place, place, 4, s)
        copy.wait_recv()
        sib_copies[s].wait_recv()
        down.append(copy)

    out = local(factors, factor_out, 0)
    for group in (block_copies, gram_copies, x_copies, sib_copies):
        for copy in group.values():
            copy.wait_send()
    for copy in down:
        copy.wait_send()
    c_est.wait()
    out.wait()


def apply_kernel(wide, estimate, correct, trend, factors, out):
    out[...] = (
        estimate[...]
        - dot_nt(correct[...], factors[:, :wide])
        - dot_nt(trend[...], factors[:, wide:])
    )


def body(
    bits_inner,
    levels,
    observed,
    leaf_order,
    leaf_inverse,
    project_basis,
    correct_basis,
    coupling,
    trend_basis,
    trend_correct,
):
    leaf, cols = observed.shape
    wide = correct_basis.shape[1]
    rank = wide // levels
    trend_rank = trend_basis.shape[1]
    held, part, rows, width = plan(cols, levels, rank, trend_rank)
    tile = 256 if leaf % 256 == 0 else leaf
    vm = pltpu.VMEM
    every = range(levels)
    scratch = [
        vm((leaf, cols), F32),
        vm((leaf, cols), BF),
        vm(leaf_order.shape, jnp.int32),
        vm((leaf, leaf), BF),
        vm((leaf, wide + trend_rank), BF),
        vm((leaf, wide), BF),
        vm((leaf, leaf), BF),
        vm((leaf, cols), F32),
        vm((cols, leaf), BF),
        vm((levels + 1,) + coupling.shape, BF),
        vm((cols, wide + trend_rank), BF),
    ]
    scratch += [vm((part[0], rows[0]), F32)]
    scratch += [vm((part[s], rows[s + 1]), F32) for s in every]
    scratch += [vm((part[s], rows[s]), BF) for s in every] * 2
    scratch += [vm((rank, width[s]), BF) for s in every] * 2
    scratch += [vm((part[s], rank), BF) for s in every]
    scratch += [
        pltpu.SemaphoreType.DMA((8,)),
        pltpu.SemaphoreType.DMA((5, levels)),
        pltpu.SemaphoreType.DMA((5, levels)),
    ]
    anywhere = pl.BlockSpec(memory_space=pl.ANY)
    estimate, factors = pl.pallas_call(
        functools.partial(sweep_kernel, bits_inner, levels, rank, tile),
        out_shape=(
            jax.ShapeDtypeStruct((leaf, cols), F32),
            jax.ShapeDtypeStruct((cols, wide + trend_rank), BF),
        ),
        in_specs=[anywhere] * 7,
        out_specs=(anywhere, anywhere),
        scratch_shapes=scratch,
        compiler_params=pltpu.CompilerParams(
            collective_id=0, has_side_effects=True, vmem_limit_bytes=56 * 1024 * 1024
        ),
        name="tree_sweep",
    )(observed, leaf_order, leaf_inverse, project_basis, correct_basis, coupling, trend_basis)
    return pl.pallas_call(
        functools.partial(apply_kernel, wide),
        grid=(leaf // tile,),
        out_shape=jax.ShapeDtypeStruct((leaf, cols), F32),
        in_specs=[
            pl.BlockSpec((tile, cols), lambda i: (i, 0)),
            pl.BlockSpec((tile, wide), lambda i: (i, 0)),
            pl.BlockSpec((tile, trend_rank), lambda i: (i, 0)),
            pl.BlockSpec((cols, wide + trend_rank), lambda i: (0, 0)),
        ],
        out_specs=pl.BlockSpec((tile, cols), lambda i: (i, 0)),
        compiler_params=pltpu.CompilerParams(vmem_limit_bytes=40 * 1024 * 1024),
        name="apply_factors",
    )(estimate, correct_basis, trend_correct, factors)


def solution(mesh):
    bits_inner = mesh.shape["inner"].bit_length() - 1
    bits_outer = mesh.shape["outer"].bit_length() - 1
    rows = P(("outer", "inner"), None)
    return jax.shard_map(
        functools.partial(body, bits_inner, bits_inner + bits_outer),
        mesh=mesh,
        in_specs=(rows,) * 8,
        out_specs=rows,
        check_vma=False,
    )
```

```python
import functools

import jax
import jax.numpy as jnp
from jax import lax
from jax.experimental import pallas as pl
from jax.experimental.pallas import tpu as pltpu
from jax.sharding import PartitionSpec as P

MESH = pl.DeviceIdType.MESH
BF = jnp.bfloat16
F32 = jnp.float32
NT = (((1,), (1,)), ((), ()))


def dot(a, b):
    return jnp.dot(a, b, preferred_element_type=F32)


def dot_nt(a, b):
    return lax.dot_general(a, b, NT, preferred_element_type=F32)


def plan(cols, levels, rank, trend):
    held, part = [], []
    now = cols
    for _ in range(levels):
        held.append(now)
        if now % 32 == 0:
            now //= 2
        part.append(now)
    rows = [(levels - s) * rank + trend for s in range(levels + 1)]
    width = [sum(rows[s + 1 :]) for s in range(levels)]
    return held, part, rows, width


def sweep_kernel(
    bits_inner,
    levels,
    rank,
    group,
    tile,
    observed,
    order,
    inverse,
    project,
    correct,
    coupling,
    trend,
    estimate_out,
    factor_out,
    obs_v,
    obs_bf,
    order_v,
    inv_v,
    basis_v,
    correct_v,
    hot_v,
    est_v,
    est_t,
    blocks,
    factors,
    gram_local,
    *rest,
):
    leaf, cols = observed.shape
    trend_rank = trend.shape[1]
    groups = cols // group
    held, part, rows, width = plan(group, levels, rank, trend_rank)
    rest = list(rest)

    def take(n):
        taken = rest[:n]
        del rest[:n]
        return taken

    sums = [take(levels + 1) for _ in range(groups)]
    x_send = [take(levels) for _ in range(groups)]
    x_recv = [take(levels) for _ in range(groups)]
    sib = [take(levels) for _ in range(groups)]
    gram = take(levels)
    gram_rest = take(levels - 1)
    gram_in = take(levels - 1)
    local_sem, send_sem, recv_sem = rest

    outer, inner = lax.axis_index("outer"), lax.axis_index("inner")
    bits, partners = [], []
    for s in range(levels):
        if s < bits_inner:
            span = 1 << s
            bit = lax.rem(inner // span, 2)
            partners.append((outer, inner + (1 - 2 * bit) * span))
        else:
            span = 1 << (s - bits_inner)
            bit = lax.rem(outer // span, 2)
            partners.append((outer + (1 - 2 * bit) * span, inner))
        bits.append(bit)
    side = bits[0]

    def local(src, dst, i):
        copy = pltpu.make_async_copy(src, dst, local_sem.at[i])
        copy.start()
        return copy

    wide = levels * rank
    c_block = local(coupling, blocks.at[0], 0)
    c_correct = local(correct, correct_v, 1)
    c_project = local(project, basis_v.at[:, pl.ds(0, wide)], 2)
    c_trend = local(trend, basis_v.at[:, pl.ds(wide, trend_rank)], 3)
    c_order = local(order, order_v, 4)
    c_inv = local(inverse, inv_v, 5)
    c_obs = local(observed, obs_v, 6)

    barrier = pltpu.get_barrier_semaphore()
    for partner in partners:
        pl.semaphore_signal(barrier, inc=1, device_id=partner, device_id_type=MESH)
    pl.semaphore_wait(barrier, levels)

    sent = []

    def remote(src, dst, kind, s, to):
        copy = pltpu.make_async_remote_copy(
            src_ref=src,
            dst_ref=dst,
            send_sem=send_sem.at[kind, s],
            recv_sem=recv_sem.at[kind, s],
            device_id=partners[to],
            device_id_type=MESH,
        )
        copy.start()
        sent.append(copy)
        return copy

    block_rows = coupling.shape[0] // 2
    gram_rows = rank // 2
    my_block = pl.ds(pl.multiple_of(side * block_rows, block_rows), block_rows)
    my_gram = pl.ds(pl.multiple_of(side * gram_rows, gram_rows), gram_rows)
    move = {}
    pending = jnp.int32(0)
    block_of = []

    def send_block(s):
        if s == 0:
            move["block", s] = remote(blocks.at[0], blocks.at[1], 0, s, s)
        else:
            place = blocks.at[s + 1, my_block]
            move["block", s] = remote(blocks.at[pending, my_block], place, 0, s, s)

    def send_gram(s):
        if s == 0:
            move["gram", s] = remote(gram[0].at[0], gram[0].at[1], 2, s, s)
            if levels > 1:
                move["rest", s] = remote(gram_local.at[1 - side], gram_in[0], 3, s, s)
            return
        mine = gram[s].at[0, my_gram]
        move["gram", s] = remote(mine, gram[s].at[1, my_gram], 2, s, s)
        if s + 1 < levels:
            move["rest", s] = remote(gram_rest[s], gram_in[s], 3, s, s)
        move["own", s] = remote(mine, mine, 4, s, 0)

    def advance(s):
        nonlocal pending
        move["block", s].wait_recv()
        block_of.append(jnp.where(bits[s] == 1, pending, s + 1))
        pending = jnp.where(bits[s] == 1, s + 1, pending)
        if s + 1 < levels:
            send_block(s + 1)
            move["rest", s].wait_recv()
            here = gram_local[side] if s == 0 else gram_rest[s][...]
            total = (here.astype(F32) + gram_in[s][...].astype(F32)).astype(BF)
            skip = rows[s + 2]
            gram[s + 1][0, my_gram, :] = total[:, :skip]
            if s + 2 < levels:
                gram_rest[s + 1][...] = total[:, skip:]
            send_gram(s + 1)
        move["gram", s].wait_recv()
        if s > 0:
            block = blocks.at[s + 1, my_block]
            move["block2", s] = remote(block, block, 1, s, 0)
            other = gram[s].at[1, my_gram]
            move["other", s] = remote(other, other, 5, s, 0)

    def ready(s):
        if s > 0:
            move["block2", s].wait_recv()
            move["own", s].wait_recv()
            move["other", s].wait_recv()

    c_block.wait()
    send_block(0)

    c_correct.wait()
    c_project.wait()
    c_trend.wait()
    at = 0
    for s in range(levels):
        columns_t = correct_v[:, s * rank : (s + 1) * rank].T
        value = dot(columns_t, basis_v[:, (s + 1) * rank :]).astype(BF)
        if s == 0:
            gram[0][0] = value
        else:
            gram_local[0, :, at : at + rows[s + 1]] = value[:gram_rows]
            gram_local[1, :, at : at + rows[s + 1]] = value[gram_rows:]
            at += rows[s + 1]
    send_gram(0)

    c_order.wait()
    steps = leaf // tile

    def make_hot(t, carry):
        r0 = pl.multiple_of(t * tile, tile)
        ids = lax.broadcasted_iota(jnp.int32, (tile, leaf), 0) + r0
        hot_v[pl.ds(r0, tile), :] = jnp.where(ids == order_v[...], 1.0, 0.0).astype(BF)
        return carry

    lax.fori_loop(0, steps, make_hot, 0)
    advance(0)
    c_inv.wait()

    def reorder(t, carry):
        r0 = pl.multiple_of(t * tile, tile)
        value = dot_nt(inv_v[pl.ds(r0, tile), :], hot_v[...]).astype(BF)
        inv_v[pl.ds(r0, tile), :] = value
        return carry

    lax.fori_loop(0, steps, reorder, 0)
    c_obs.wait()

    x_move, sib_move, down_move = {}, {}, {}
    offsets = [[jnp.int32(g * group)] for g in range(groups)]
    finals = []

    def send_x(g, s):
        x_move[g, s] = remote(x_send[g][s], x_recv[g][s], 6 + g, s, s)

    def start_group(g):
        lanes = slice(g * group, (g + 1) * group)

        def make_estimate(t, carry):
            r0 = pl.multiple_of(t * tile, tile)
            value = dot(inv_v[pl.ds(r0, tile), :], obs_bf[:, lanes])
            est_v[pl.ds(r0, tile), lanes] = value
            est_t[lanes, pl.ds(r0, tile)] = value.astype(BF).T
            return carry

        obs_bf[:, lanes] = obs_v[:, lanes].astype(BF)
        lax.fori_loop(0, steps, make_estimate, 0)
        half = part[0]
        away = pl.ds(pl.multiple_of(g * group + (1 - side) * half, half), half)
        x_send[g][0][...] = dot(est_t[away, :], basis_v[...]).astype(BF)
        send_x(g, 0)
        keep = pl.ds(pl.multiple_of(g * group + side * half, half), half)
        sums[g][0][...] = dot(est_t[keep, :], basis_v[...])

    def up(g, s):
        count = part[s]
        halves = held[s] != part[s]
        first_side = bits[s] == 0
        offset = offsets[g][s] + (bits[s] * count if halves else 0)
        offset = pl.multiple_of(offset, count)
        offsets[g].append(offset)
        if s == 0 or not halves:
            own = sums[g][s][...]
        else:
            own = sums[g][s][pl.ds(pl.multiple_of(bits[s] * count, count), count), :]
        x_move[g, s].wait_recv()
        if g == 0:
            ready(s)
        other = x_recv[g][s][...].astype(F32)
        own_head, other_head = own[:, :rank], other[:, :rank]
        one = jnp.where(first_side, own_head, other_head).astype(BF)
        two = jnp.where(first_side, other_head, own_head).astype(BF)
        block = blocks[block_of[s]]
        factor = dot_nt(one, block[:, :rank]) + dot_nt(two, block[:, rank:])
        mine = jnp.where(first_side, factor[:, :rank], factor[:, rank:]).astype(BF)
        theirs = jnp.where(first_side, factor[:, rank:], factor[:, :rank]).astype(BF)
        new = (
            own[:, rank:]
            + other[:, rank:]
            - dot(mine, gram[s][0])
            - dot(theirs, gram[s][1])
        )
        sums[g][s + 1][...] = new
        if s + 1 < levels:
            after = part[s + 1]
            if held[s + 1] != after:
                away = pl.multiple_of((1 - bits[s + 1]) * after, after)
                x_send[g][s + 1][...] = sums[g][s + 1][pl.ds(away, after), :].astype(BF)
            else:
                x_send[g][s + 1][...] = new.astype(BF)
            send_x(g, s + 1)
        factors[pl.ds(offset, count), s * rank : (s + 1) * rank] = mine
        if halves:
            sib[g][s][...] = theirs
            place = factors.at[pl.ds(offset, count), pl.ds(s * rank, rank)]
            sib_move[g, s] = remote(sib[g][s], place, 6 + groups + g, s, s)
        if s + 1 == levels:
            trend_factor = dot_nt(new.astype(BF), blocks[pending]).astype(BF)
            factors[pl.ds(offset, count), wide:] = trend_factor
            send_down(g, 0)

    split = [s for s in reversed(range(levels)) if held[s] != part[s]]

    def send_down(g, i):
        s = split[i]
        lanes = pl.ds((s + 1) * rank, rows[s + 1])
        place = factors.at[pl.ds(offsets[g][s + 1], part[s]), lanes]
        down_move[g, i] = remote(place, place, 6 + 2 * groups + g, s, s)

    def down(g, i):
        down_move[g, i].wait_recv()
        sib_move[g, split[i]].wait_recv()
        if i + 1 < len(split):
            send_down(g, i + 1)
        else:
            mine = pl.ds(g * group, group)
            finals.append(local(factors.at[mine], factor_out.at[mine], 8 + g))

    last = 1 + levels + len(split)
    for wave in range(last + groups - 1):
        for g in reversed(range(groups)):
            step = wave - g
            if step < 0 or step >= last:
                continue
            if step == 0:
                start_group(g)
                if g == groups - 1:
                    finals.append(local(est_v, estimate_out, 7))
            elif step <= levels:
                if g == 0 and step > 1:
                    advance(step - 1)
                up(g, step - 1)
            else:
                down(g, step - 1 - levels)

    for copy in sent:
        copy.wait_send()
    for copy in finals:
        copy.wait()


def apply_kernel(wide, estimate, correct, trend, factors, out):
    out[...] = (
        estimate[...]
        - dot_nt(correct[...], factors[:, :wide])
        - dot_nt(trend[...], factors[:, wide:])
    )


def body(
    bits_inner,
    levels,
    observed,
    leaf_order,
    leaf_inverse,
    project_basis,
    correct_basis,
    coupling,
    trend_basis,
    trend_correct,
):
    leaf, cols = observed.shape
    wide = correct_basis.shape[1]
    rank = wide // levels
    trend_rank = trend_basis.shape[1]
    group = 256 if cols % 256 == 0 else cols
    groups = cols // group
    held, part, rows, width = plan(group, levels, rank, trend_rank)
    tile = 256 if leaf % 256 == 0 else leaf
    vm = pltpu.VMEM
    every = range(levels)
    scratch = [
        vm((leaf, cols), F32),
        vm((leaf, cols), BF),
        vm(leaf_order.shape, jnp.int32),
        vm((leaf, leaf), BF),
        vm((leaf, wide + trend_rank), BF),
        vm((leaf, wide), BF),
        vm((leaf, leaf), BF),
        vm((leaf, cols), F32),
        vm((cols, leaf), BF),
        vm((levels + 1,) + coupling.shape, BF),
        vm((cols, wide + trend_rank), BF),
        vm((2, rank // 2, max(width[0] - rows[1], rank)), BF),
    ]
    for _ in range(groups):
        scratch += [vm((part[0], rows[0]), F32)]
        scratch += [vm((part[s], rows[s + 1]), F32) for s in every]
    scratch += [vm((part[s], rows[s]), BF) for s in every] * (2 * groups)
    scratch += [vm((part[s], rank), BF) for s in every] * groups
    scratch += [vm((2, rank, rows[s + 1]), BF) for s in every]
    scratch += [vm((rank // 2, width[s + 1]), BF) for s in range(levels - 1)] * 2
    scratch += [
        pltpu.SemaphoreType.DMA((8 + groups,)),
        pltpu.SemaphoreType.DMA((6 + 3 * groups, levels)),
        pltpu.SemaphoreType.DMA((6 + 3 * groups, levels)),
    ]
    anywhere = pl.BlockSpec(memory_space=pl.ANY)
    estimate, factors = pl.pallas_call(
        functools.partial(sweep_kernel, bits_inner, levels, rank, group, tile),
        out_shape=(
            jax.ShapeDtypeStruct((leaf, cols), F32),
            jax.ShapeDtypeStruct((cols, wide + trend_rank), BF),
        ),
        in_specs=[anywhere] * 7,
        out_specs=(anywhere, anywhere),
        scratch_shapes=scratch,
        compiler_params=pltpu.CompilerParams(
            collective_id=0, has_side_effects=True, vmem_limit_bytes=56 * 1024 * 1024
        ),
        name="tree_sweep",
    )(observed, leaf_order, leaf_inverse, project_basis, correct_basis, coupling, trend_basis)
    return pl.pallas_call(
        functools.partial(apply_kernel, wide),
        grid=(leaf // tile,),
        out_shape=jax.ShapeDtypeStruct((leaf, cols), F32),
        in_specs=[
            pl.BlockSpec((tile, cols), lambda i: (i, 0)),
            pl.BlockSpec((tile, wide), lambda i: (i, 0)),
            pl.BlockSpec((tile, trend_rank), lambda i: (i, 0)),
            pl.BlockSpec((cols, wide + trend_rank), lambda i: (0, 0)),
        ],
        out_specs=pl.BlockSpec((tile, cols), lambda i: (i, 0)),
        compiler_params=pltpu.CompilerParams(vmem_limit_bytes=62 * 1024 * 1024),
        name="apply_factors",
    )(estimate, correct_basis, trend_correct, factors)


def solution(mesh):
    bits_inner = mesh.shape["inner"].bit_length() - 1
    bits_outer = mesh.shape["outer"].bit_length() - 1
    rows = P(("outer", "inner"), None)
    return jax.shard_map(
        functools.partial(body, bits_inner, bits_inner + bits_outer),
        mesh=mesh,
        in_specs=(rows,) * 8,
        out_specs=rows,
        check_vma=False,
    )
```

```python
import functools

import jax
import jax.numpy as jnp
from jax import lax
from jax.experimental import pallas as pl
from jax.experimental.pallas import tpu as pltpu
from jax.sharding import PartitionSpec as P

MESH = pl.DeviceIdType.MESH
BF = jnp.bfloat16
F32 = jnp.float32
NT = (((1,), (1,)), ((), ()))


def dot(a, b):
    return jnp.dot(a, b, preferred_element_type=F32)


def dot_nt(a, b):
    return lax.dot_general(a, b, NT, preferred_element_type=F32)


def plan(cols, levels, rank, trend):
    held, part = [], []
    now = cols
    for _ in range(levels):
        held.append(now)
        if now % 32 == 0:
            now //= 2
        part.append(now)
    rows = [(levels - s) * rank + trend for s in range(levels + 1)]
    width = [sum(rows[s + 1 :]) for s in range(levels)]
    return held, part, rows, width


def sweep_kernel(
    bits_inner,
    levels,
    rank,
    group,
    tile,
    observed,
    order,
    inverse,
    project,
    correct,
    coupling,
    trend,
    trend_correct,
    out,
    obs_v,
    obs_bf,
    order_v,
    inv_v,
    basis_v,
    correct_v,
    trend_v,
    hot_v,
    est_v,
    est_t,
    blocks,
    factors,
    gram_local,
    *rest,
):
    leaf, cols = observed.shape
    trend_rank = trend.shape[1]
    groups = cols // group
    held, part, rows, width = plan(group, levels, rank, trend_rank)
    rest = list(rest)

    def take(n):
        taken = rest[:n]
        del rest[:n]
        return taken

    sums = [take(levels + 1) for _ in range(groups)]
    x_send = [take(levels) for _ in range(groups)]
    x_recv = [take(levels) for _ in range(groups)]
    sib = [take(levels) for _ in range(groups)]
    gram = take(levels)
    gram_rest = take(levels - 1)
    gram_in = take(levels - 1)
    local_sem, send_sem, recv_sem = rest

    outer, inner = lax.axis_index("outer"), lax.axis_index("inner")
    bits, partners = [], []
    for s in range(levels):
        if s < bits_inner:
            span = 1 << s
            bit = lax.rem(inner // span, 2)
            partners.append((outer, inner + (1 - 2 * bit) * span))
        else:
            span = 1 << (s - bits_inner)
            bit = lax.rem(outer // span, 2)
            partners.append((outer + (1 - 2 * bit) * span, inner))
        bits.append(bit)
    side = bits[0]

    def local(src, dst, i):
        copy = pltpu.make_async_copy(src, dst, local_sem.at[i])
        copy.start()
        return copy

    wide = levels * rank
    c_block = local(coupling, blocks.at[0], 0)
    c_correct = local(correct, correct_v, 1)
    c_project = local(project, basis_v.at[:, pl.ds(0, wide)], 2)
    c_trend = local(trend, basis_v.at[:, pl.ds(wide, trend_rank)], 3)
    c_order = local(order, order_v, 4)

    barrier = pltpu.get_barrier_semaphore()
    for partner in partners:
        pl.semaphore_signal(barrier, inc=1, device_id=partner, device_id_type=MESH)
    pl.semaphore_wait(barrier, levels)

    sent = []

    def remote(src, dst, kind, s, to):
        copy = pltpu.make_async_remote_copy(
            src_ref=src,
            dst_ref=dst,
            send_sem=send_sem.at[kind, s],
            recv_sem=recv_sem.at[kind, s],
            device_id=partners[to],
            device_id_type=MESH,
        )
        copy.start()
        sent.append(copy)
        return copy

    block_rows = coupling.shape[0] // 2
    gram_rows = rank // 2
    my_block = pl.ds(pl.multiple_of(side * block_rows, block_rows), block_rows)
    my_gram = pl.ds(pl.multiple_of(side * gram_rows, gram_rows), gram_rows)
    move = {}
    pending = jnp.int32(0)
    block_of = []

    def send_block(s):
        if s == 0:
            move["block", s] = remote(blocks.at[0], blocks.at[1], 0, s, s)
        else:
            place = blocks.at[s + 1, my_block]
            move["block", s] = remote(blocks.at[pending, my_block], place, 0, s, s)

    def send_gram(s):
        if s == 0:
            if levels > 1:
                move["rest", s] = remote(gram_local.at[1 - side], gram_in[0], 3, s, s)
            move["gram", s] = remote(gram[0].at[0], gram[0].at[1], 2, s, s)
            return
        if s + 1 < levels:
            move["rest", s] = remote(gram_rest[s], gram_in[s], 3, s, s)
        mine = gram[s].at[0, my_gram]
        move["gram", s] = remote(mine, gram[s].at[1, my_gram], 2, s, s)
        move["own", s] = remote(mine, mine, 4, s, 0)

    def advance_block(s):
        nonlocal pending
        move["block", s].wait_recv()
        block_of.append(jnp.where(bits[s] == 1, pending, s + 1))
        pending = jnp.where(bits[s] == 1, s + 1, pending)
        if s + 1 < levels:
            send_block(s + 1)
        if s > 0:
            block = blocks.at[s + 1, my_block]
            move["block2", s] = remote(block, block, 1, s, 0)

    def advance_gram(s):
        if s + 1 >= levels:
            return
        move["rest", s].wait_recv()
        here = gram_local[side] if s == 0 else gram_rest[s][...]
        total = (here.astype(F32) + gram_in[s][...].astype(F32)).astype(BF)
        skip = rows[s + 2]
        if s + 2 < levels:
            gram_rest[s + 1][...] = total[:, skip:]
        gram[s + 1][0, my_gram, :] = total[:, :skip]
        send_gram(s + 1)

    def share_gram(s):
        move["gram", s].wait_recv()
        if s > 0:
            other = gram[s].at[1, my_gram]
            move["other", s] = remote(other, other, 5, s, 0)

    def ready(s):
        if s > 0:
            move["block2", s].wait_recv()
            move["own", s].wait_recv()
            move["other", s].wait_recv()

    c_block.wait()
    send_block(0)

    c_correct.wait()
    c_project.wait()
    c_trend.wait()
    c_inv = local(inverse, inv_v, 5)
    c_obs = local(observed, obs_v, 6)
    c_last = local(trend_correct, trend_v, 7)
    at = 0
    for s in range(0, levels, 2):
        both = min(2, levels - s)
        columns_t = correct_v[:, s * rank : (s + both) * rank].T
        pair = dot(columns_t, basis_v[:, (s + 1) * rank :]).astype(BF)
        for u in range(both):
            value = pair[u * rank : (u + 1) * rank, u * rank :]
            if s + u == 0:
                gram[0][0] = value
            else:
                gram_local[0, :, at : at + rows[s + u + 1]] = value[:gram_rows]
                gram_local[1, :, at : at + rows[s + u + 1]] = value[gram_rows:]
                at += rows[s + u + 1]
    send_gram(0)
    advance_block(0)

    c_order.wait()
    steps = leaf // tile

    def make_hot(t, carry):
        r0 = pl.multiple_of(t * tile, tile)
        ids = lax.broadcasted_iota(jnp.int32, (tile, leaf), 0) + r0
        hot_v[pl.ds(r0, tile), :] = jnp.where(ids == order_v[...], 1.0, 0.0).astype(BF)
        return carry

    lax.fori_loop(0, steps, make_hot, 0)
    advance_gram(0)
    c_inv.wait()

    def reorder(t, carry):
        r0 = pl.multiple_of(t * tile, tile)
        value = dot_nt(inv_v[pl.ds(r0, tile), :], hot_v[...]).astype(BF)
        inv_v[pl.ds(r0, tile), :] = value
        return carry

    lax.fori_loop(0, steps, reorder, 0)
    if levels > 1:
        advance_block(1)
    c_obs.wait()
    c_last.wait()

    x_move, sib_move, down_move = {}, {}, {}
    offsets = [[jnp.int32(g * group)] for g in range(groups)]
    finals = []

    def send_x(g, s):
        x_move[g, s] = remote(x_send[g][s], x_recv[g][s], 6 + g, s, s)

    def start_group(g):
        lanes = slice(g * group, (g + 1) * group)

        def make_estimate(t, carry):
            r0 = pl.multiple_of(t * tile, tile)
            value = dot(inv_v[pl.ds(r0, tile), :], obs_bf[:, lanes])
            est_v[pl.ds(r0, tile), lanes] = value
            est_t[lanes, pl.ds(r0, tile)] = value.astype(BF).T
            return carry

        obs_bf[:, lanes] = obs_v[:, lanes].astype(BF)
        lax.fori_loop(0, steps, make_estimate, 0)
        sums[g][0][...] = dot(est_t[lanes, :], basis_v[...])
        if held[0] != part[0]:
            away = pl.ds(pl.multiple_of((1 - side) * part[0], part[0]), part[0])
            x_send[g][0][...] = sums[g][0][away, :].astype(BF)
        else:
            x_send[g][0][...] = sums[g][0][...].astype(BF)
        send_x(g, 0)

    def up(g, s):
        count = part[s]
        halves = held[s] != part[s]
        first_side = bits[s] == 0
        offset = offsets[g][s] + (bits[s] * count if halves else 0)
        offset = pl.multiple_of(offset, count)
        offsets[g].append(offset)
        if not halves:
            own = sums[g][s][...]
        else:
            own = sums[g][s][pl.ds(pl.multiple_of(bits[s] * count, count), count), :]
        x_move[g, s].wait_recv()
        if g == 0:
            ready(s)
        other = x_recv[g][s][...].astype(F32)
        own_head, other_head = own[:, :rank], other[:, :rank]
        one = jnp.where(first_side, own_head, other_head).astype(BF)
        two = jnp.where(first_side, other_head, own_head).astype(BF)
        block = blocks[block_of[s]]
        factor = dot_nt(one, block[:, :rank]) + dot_nt(two, block[:, rank:])
        mine = jnp.where(first_side, factor[:, :rank], factor[:, rank:]).astype(BF)
        theirs = jnp.where(first_side, factor[:, rank:], factor[:, :rank]).astype(BF)
        new = (
            own[:, rank:]
            + other[:, rank:]
            - dot(mine, gram[s][0])
            - dot(theirs, gram[s][1])
        )
        sums[g][s + 1][...] = new
        if s + 1 < levels:
            after = part[s + 1]
            if held[s + 1] != after:
                away = pl.multiple_of((1 - bits[s + 1]) * after, after)
                x_send[g][s + 1][...] = sums[g][s + 1][pl.ds(away, after), :].astype(BF)
            else:
                x_send[g][s + 1][...] = new.astype(BF)
            send_x(g, s + 1)
        factors[pl.ds(offset, count), s * rank : (s + 1) * rank] = mine
        if halves:
            sib[g][s][...] = theirs
            place = factors.at[pl.ds(offset, count), pl.ds(s * rank, rank)]
            sib_move[g, s] = remote(sib[g][s], place, 6 + groups + g, s, s)
        if s + 1 == levels:
            trend_factor = dot_nt(new.astype(BF), blocks[pending]).astype(BF)
            factors[pl.ds(offset, count), wide:] = trend_factor
            send_down(g, 0)

    split = [s for s in reversed(range(levels)) if held[s] != part[s]]

    def send_down(g, i):
        s = split[i]
        lanes = pl.ds((s + 1) * rank, rows[s + 1])
        place = factors.at[pl.ds(offsets[g][s + 1], part[s]), lanes]
        down_move[g, i] = remote(place, place, 6 + 2 * groups + g, s, s)

    def down(g, i):
        down_move[g, i].wait_recv()
        sib_move[g, split[i]].wait_recv()
        if i + 1 < len(split):
            send_down(g, i + 1)
        else:
            finish(g)

    def finish(g):
        lanes = slice(g * group, (g + 1) * group)

        def apply(t, carry):
            r0 = pl.multiple_of(t * tile, tile)
            place = pl.ds(r0, tile)
            est_v[place, lanes] = (
                est_v[place, lanes]
                - dot_nt(correct_v[place, :], factors[lanes, :wide])
                - dot_nt(trend_v[place, :], factors[lanes, wide:])
            )
            return carry

        lax.fori_loop(0, steps, apply, 0)
        mine = pl.ds(g * group, group)
        finals.append(local(est_v.at[:, mine], out.at[:, mine], 8 + g))

    last = 1 + levels + len(split)
    for wave in range(last + groups - 1):
        for g in reversed(range(groups)):
            step = wave - g
            if step < 0 or step >= last:
                continue
            if step == 0:
                start_group(g)
            elif step <= levels:
                if g == 0:
                    if step + 1 < levels:
                        advance_block(step + 1)
                    if step < levels:
                        advance_gram(step)
                    if step == 1:
                        share_gram(0)
                up(g, step - 1)
                if g == 0 and step < levels:
                    share_gram(step)
            else:
                down(g, step - 1 - levels)

    for copy in sent:
        copy.wait_send()
    for copy in finals:
        copy.wait()


def body(
    bits_inner,
    levels,
    observed,
    leaf_order,
    leaf_inverse,
    project_basis,
    correct_basis,
    coupling,
    trend_basis,
    trend_correct,
):
    leaf, cols = observed.shape
    wide = correct_basis.shape[1]
    rank = wide // levels
    trend_rank = trend_basis.shape[1]
    group = 256 if cols % 256 == 0 else cols
    groups = cols // group
    held, part, rows, width = plan(group, levels, rank, trend_rank)
    tile = 512 if leaf % 512 == 0 else leaf
    vm = pltpu.VMEM
    every = range(levels)
    scratch = [
        vm((leaf, cols), F32),
        vm((leaf, cols), BF),
        vm(leaf_order.shape, jnp.int32),
        vm((leaf, leaf), BF),
        vm((leaf, wide + trend_rank), BF),
        vm((leaf, wide), BF),
        vm((leaf, trend_rank), BF),
        vm((leaf, leaf), BF),
        vm((leaf, cols), F32),
        vm((cols, leaf), BF),
        vm((levels + 1,) + coupling.shape, BF),
        vm((cols, wide + trend_rank), BF),
        vm((2, rank // 2, max(width[0] - rows[1], rank)), BF),
    ]
    for _ in range(groups):
        scratch += [vm((held[0], rows[0]), F32)]
        scratch += [vm((part[s], rows[s + 1]), F32) for s in every]
    scratch += [vm((part[s], rows[s]), BF) for s in every] * (2 * groups)
    scratch += [vm((part[s], rank), BF) for s in every] * groups
    scratch += [vm((2, rank, rows[s + 1]), BF) for s in every]
    scratch += [vm((rank // 2, width[s + 1]), BF) for s in range(levels - 1)] * 2
    scratch += [
        pltpu.SemaphoreType.DMA((8 + groups,)),
        pltpu.SemaphoreType.DMA((6 + 3 * groups, levels)),
        pltpu.SemaphoreType.DMA((6 + 3 * groups, levels)),
    ]
    return pl.pallas_call(
        functools.partial(sweep_kernel, bits_inner, levels, rank, group, tile),
        out_shape=jax.ShapeDtypeStruct((leaf, cols), F32),
        in_specs=[pl.BlockSpec(memory_space=pltpu.HBM)] * 8,
        out_specs=pl.BlockSpec(memory_space=pl.ANY),
        scratch_shapes=scratch,
        compiler_params=pltpu.CompilerParams(
            collective_id=0, has_side_effects=True, vmem_limit_bytes=56 * 1024 * 1024
        ),
        name="tree_sweep",
    )(
        observed,
        leaf_order,
        leaf_inverse,
        project_basis,
        correct_basis,
        coupling,
        trend_basis,
        trend_correct,
    )


def solution(mesh):
    bits_inner = mesh.shape["inner"].bit_length() - 1
    bits_outer = mesh.shape["outer"].bit_length() - 1
    rows = P(("outer", "inner"), None)
    return jax.shard_map(
        functools.partial(body, bits_inner, bits_inner + bits_outer),
        mesh=mesh,
        in_specs=(rows,) * 8,
        out_specs=rows,
        check_vma=False,
    )
```

```python
import functools

import jax
import jax.numpy as jnp
from jax import lax
from jax.experimental import pallas as pl
from jax.experimental.pallas import tpu as pltpu
from jax.sharding import PartitionSpec as P

MESH = pl.DeviceIdType.MESH
BF = jnp.bfloat16
F32 = jnp.float32
NT = (((1,), (1,)), ((), ()))


def dot(a, b):
    return jnp.dot(a, b, preferred_element_type=F32)


def dot_nt(a, b):
    return lax.dot_general(a, b, NT, preferred_element_type=F32)


def plan(cols, levels, rank, trend):
    held, part = [], []
    now = cols
    for _ in range(levels):
        held.append(now)
        if now % 32 == 0:
            now //= 2
        part.append(now)
    rows = [(levels - s) * rank + trend for s in range(levels + 1)]
    width = [sum(rows[s + 1 :]) for s in range(levels)]
    return held, part, rows, width


def sweep_kernel(
    bits_inner,
    levels,
    rank,
    group,
    tile,
    observed,
    order,
    inverse,
    project,
    correct,
    coupling,
    trend,
    trend_correct,
    out,
    obs_v,
    obs_bf,
    order_v,
    inv_v,
    basis_v,
    correct_v,
    trend_v,
    hot_v,
    column_v,
    ordered_v,
    est_v,
    est_t,
    blocks,
    factors,
    gram_local,
    *rest,
):
    leaf, cols = observed.shape
    trend_rank = trend.shape[1]
    groups = cols // group
    held, part, rows, width = plan(group, levels, rank, trend_rank)
    rest = list(rest)

    def take(n):
        taken = rest[:n]
        del rest[:n]
        return taken

    sums = [take(levels + 1) for _ in range(groups)]
    x_send = [take(levels) for _ in range(groups)]
    x_recv = [take(levels) for _ in range(groups)]
    sib = [take(levels) for _ in range(groups)]
    gram = take(levels)
    gram_rest = take(levels - 1)
    gram_in = take(levels - 1)
    local_sem, send_sem, recv_sem = rest

    outer, inner = lax.axis_index("outer"), lax.axis_index("inner")
    bits, partners = [], []
    for s in range(levels):
        if s < bits_inner:
            span = 1 << s
            bit = lax.rem(inner // span, 2)
            partners.append((outer, inner + (1 - 2 * bit) * span))
        else:
            span = 1 << (s - bits_inner)
            bit = lax.rem(outer // span, 2)
            partners.append((outer + (1 - 2 * bit) * span, inner))
        bits.append(bit)
    side = bits[0]
    split = [s for s in range(levels) if held[s] != part[s]]
    late = len(split)

    def across(mask):
        to_outer, to_inner = outer, inner
        for s in range(levels):
            if mask >> s & 1:
                if s < bits_inner:
                    to_inner = to_inner + (1 - 2 * bits[s]) * (1 << s)
                else:
                    to_outer = to_outer + (1 - 2 * bits[s]) * (1 << (s - bits_inner))
        return to_outer, to_inner

    wide_masks = [m for m in range(2, 1 << late, 2)]
    partners = {1 << s: partners[s] for s in range(levels)}
    for mask in wide_masks:
        partners.setdefault(mask, across(mask))

    def local(src, dst, i):
        copy = pltpu.make_async_copy(src, dst, local_sem.at[i])
        copy.start()
        return copy

    wide = levels * rank
    c_block = local(coupling, blocks.at[0], 0)
    c_correct = local(correct, correct_v, 1)
    c_project = local(project, basis_v.at[:, pl.ds(0, wide)], 2)
    c_trend = local(trend, basis_v.at[:, pl.ds(wide, trend_rank)], 3)
    c_order = local(order, order_v, 4)

    barrier = pltpu.get_barrier_semaphore()
    for partner in partners.values():
        pl.semaphore_signal(barrier, inc=1, device_id=partner, device_id_type=MESH)
    pl.semaphore_wait(barrier, len(partners))

    sent = []

    def remote(src, dst, mask):
        slot = len(sent)
        copy = pltpu.make_async_remote_copy(
            src_ref=src,
            dst_ref=dst,
            send_sem=send_sem.at[slot],
            recv_sem=recv_sem.at[slot],
            device_id=partners[mask],
            device_id_type=MESH,
        )
        copy.start()
        sent.append(copy)
        return copy

    block_rows = coupling.shape[0] // 2
    gram_rows = rank // 2
    my_block = pl.ds(pl.multiple_of(side * block_rows, block_rows), block_rows)
    my_gram = pl.ds(pl.multiple_of(side * gram_rows, gram_rows), gram_rows)
    move = {}
    pending = jnp.int32(0)
    block_of = []

    def send_block(s):
        if s == 0:
            move["block", s] = remote(blocks.at[0], blocks.at[1], 1)
        else:
            place = blocks.at[s + 1, my_block]
            move["block", s] = remote(blocks.at[pending, my_block], place, 1 << s)

    def send_gram(s):
        if s == 0:
            if levels > 1:
                move["rest", s] = remote(gram_local.at[1 - side], gram_in[0], 1)
            move["gram", s] = remote(gram[0].at[0], gram[0].at[1], 1)
            return
        if s + 1 < levels:
            move["rest", s] = remote(gram_rest[s], gram_in[s], 1 << s)
        mine = gram[s].at[0, my_gram]
        move["gram", s] = remote(mine, gram[s].at[1, my_gram], 1 << s)
        move["own", s] = remote(mine, mine, 1)

    def advance_block(s):
        nonlocal pending
        move["block", s].wait_recv()
        block_of.append(jnp.where(bits[s] == 1, pending, s + 1))
        pending = jnp.where(bits[s] == 1, s + 1, pending)
        if s + 1 < levels:
            send_block(s + 1)
        if s > 0:
            block = blocks.at[s + 1, my_block]
            move["block2", s] = remote(block, block, 1)

    def advance_gram(s):
        if s + 1 >= levels:
            return
        move["rest", s].wait_recv()
        here = gram_local[side] if s == 0 else gram_rest[s][...]
        total = (here.astype(F32) + gram_in[s][...].astype(F32)).astype(BF)
        skip = rows[s + 2]
        if s + 2 < levels:
            gram_rest[s + 1][...] = total[:, skip:]
        gram[s + 1][0, my_gram, :] = total[:, :skip]
        send_gram(s + 1)

    def share_gram(s):
        move["gram", s].wait_recv()
        if s > 0:
            other = gram[s].at[1, my_gram]
            move["other", s] = remote(other, other, 1)

    def ready(s):
        if s > 0:
            move["block2", s].wait_recv()
            move["own", s].wait_recv()
            move["other", s].wait_recv()

    c_block.wait()
    send_block(0)

    c_correct.wait()
    c_project.wait()
    c_trend.wait()
    c_inv = local(inverse, inv_v, 5)
    c_obs = local(observed, obs_v, 6)
    c_last = local(trend_correct, trend_v, 7)
    at = 0
    for s in range(0, levels, 2):
        both = min(2, levels - s)
        columns_t = correct_v[:, s * rank : (s + both) * rank].T
        pair = dot(columns_t, basis_v[:, (s + 1) * rank :]).astype(BF)
        for u in range(both):
            value = pair[u * rank : (u + 1) * rank, u * rank :]
            if s + u == 0:
                gram[0][0] = value
            else:
                gram_local[0, :, at : at + rows[s + u + 1]] = value[:gram_rows]
                gram_local[1, :, at : at + rows[s + u + 1]] = value[gram_rows:]
                at += rows[s + u + 1]
    send_gram(0)
    advance_block(0)

    c_order.wait()
    steps = leaf // tile
    column_v[...] = jnp.broadcast_to(order_v[...].astype(F32), (128, leaf)).T
    blocks_wide = leaf // 128

    def make_hot(t, carry):
        place = pl.ds(pl.multiple_of(t * 128, 128), 128)
        column = column_v[place, :]
        lane = lax.broadcasted_iota(jnp.int32, (128, 128), 1).astype(F32)
        for k in range(blocks_wide):
            hit = column == lane + float(128 * k)
            hot_v[place, k * 128 : (k + 1) * 128] = jnp.where(hit, 1.0, 0.0).astype(BF)
        return carry

    lax.fori_loop(0, blocks_wide, make_hot, 0)
    advance_gram(0)
    c_inv.wait()

    if levels > 1:
        advance_block(1)
    c_obs.wait()
    c_last.wait()

    x_move, early, late_move, core_move = {}, {}, {}, {}
    offsets = [[jnp.int32(g * group)] for g in range(groups)]
    finals = []

    def send_x(g, s):
        x_move[g, s] = remote(x_send[g][s], x_recv[g][s], 1 << s)

    def start_group(g):
        lanes = slice(g * group, (g + 1) * group)

        def make_ordered(t, carry):
            r0 = pl.multiple_of(t * tile, tile)
            value = dot(hot_v[pl.ds(r0, tile), :], obs_bf[:, lanes])
            ordered_v[pl.ds(r0, tile), :] = value.astype(BF)
            return carry

        def make_estimate(t, carry):
            r0 = pl.multiple_of(t * tile, tile)
            value = dot(inv_v[pl.ds(r0, tile), :], ordered_v[...])
            est_v[pl.ds(r0, tile), lanes] = value
            est_t[lanes, pl.ds(r0, tile)] = value.astype(BF).T
            return carry

        obs_bf[:, lanes] = obs_v[:, lanes].astype(BF)
        lax.fori_loop(0, steps, make_ordered, 0)
        lax.fori_loop(0, steps, make_estimate, 0)
        sums[g][0][...] = dot(est_t[lanes, :], basis_v[...])
        if held[0] != part[0]:
            away = pl.ds(pl.multiple_of((1 - side) * part[0], part[0]), part[0])
            x_send[g][0][...] = sums[g][0][away, :].astype(BF)
        else:
            x_send[g][0][...] = sums[g][0][...].astype(BF)
        send_x(g, 0)

    def up(g, s):
        count = part[s]
        halves = held[s] != part[s]
        first_side = bits[s] == 0
        offset = offsets[g][s] + (bits[s] * count if halves else 0)
        offset = pl.multiple_of(offset, count)
        offsets[g].append(offset)
        if not halves:
            own = sums[g][s][...]
        else:
            own = sums[g][s][pl.ds(pl.multiple_of(bits[s] * count, count), count), :]
        x_move[g, s].wait_recv()
        if g == 0:
            ready(s)
        other = x_recv[g][s][...].astype(F32)
        own_head, other_head = own[:, :rank], other[:, :rank]
        one = jnp.where(first_side, own_head, other_head).astype(BF)
        two = jnp.where(first_side, other_head, own_head).astype(BF)
        block = blocks[block_of[s]]
        factor = dot_nt(one, block[:, :rank]) + dot_nt(two, block[:, rank:])
        mine = jnp.where(first_side, factor[:, :rank], factor[:, rank:]).astype(BF)
        theirs = jnp.where(first_side, factor[:, rank:], factor[:, :rank]).astype(BF)
        new = (
            own[:, rank:]
            + other[:, rank:]
            - dot(mine, gram[s][0])
            - dot(theirs, gram[s][1])
        )
        sums[g][s + 1][...] = new
        if s + 1 < levels:
            after = part[s + 1]
            if held[s + 1] != after:
                away = pl.multiple_of((1 - bits[s + 1]) * after, after)
                x_send[g][s + 1][...] = sums[g][s + 1][pl.ds(away, after), :].astype(BF)
            else:
                x_send[g][s + 1][...] = new.astype(BF)
            send_x(g, s + 1)
        factors[pl.ds(offset, count), s * rank : (s + 1) * rank] = mine
        if halves:
            sib[g][s][...] = theirs
        if s + 1 == levels:
            trend_factor = dot_nt(new.astype(BF), blocks[pending]).astype(BF)
            factors[pl.ds(offset, count), wide:] = trend_factor
            place = factors.at[pl.ds(offset, count), pl.ds(late * rank, rows[late])]
            for mask in wide_masks:
                late_move[g, mask] = remote(place, place, mask)
        if halves:
            place = factors.at[pl.ds(offset, count), pl.ds(s * rank, rank)]
            masks = [1] if s == 0 else [m for m in wide_masks if m < 2 << s]
            for mask in masks:
                source = sib[g][s] if mask >> s & 1 else place
                early[g, s, mask] = remote(source, place, mask)

    def core_rows(g):
        return pl.ds(pl.multiple_of(g * group + side * part[0], part[0]), part[0])

    def share_early(g):
        for s in split[1:]:
            for mask in wide_masks:
                if (g, s, mask) in early:
                    early[g, s, mask].wait_recv()
        if late > 1:
            place = factors.at[core_rows(g), pl.ds(rank, (late - 1) * rank)]
            core_move[g, 0] = remote(place, place, 1)

    def share_late(g):
        for mask in wide_masks:
            late_move[g, mask].wait_recv()
        place = factors.at[core_rows(g), pl.ds(late * rank, rows[late])]
        core_move[g, 1] = remote(place, place, 1)

    def end_group(g):
        early[g, 0, 1].wait_recv()
        if late > 1:
            core_move[g, 0].wait_recv()
        core_move[g, 1].wait_recv()
        finish(g)

    def finish(g):
        lanes = slice(g * group, (g + 1) * group)

        def apply(t, carry):
            r0 = pl.multiple_of(t * tile, tile)
            place = pl.ds(r0, tile)
            est_v[place, lanes] = (
                est_v[place, lanes]
                - dot_nt(correct_v[place, :], factors[lanes, :wide])
                - dot_nt(trend_v[place, :], factors[lanes, wide:])
            )
            return carry

        lax.fori_loop(0, steps, apply, 0)
        mine = pl.ds(g * group, group)
        finals.append(local(est_v.at[:, mine], out.at[:, mine], 8 + g))

    last = 3 + levels
    for wave in range(last + groups - 1):
        for g in reversed(range(groups)):
            step = wave - g
            if step < 0 or step >= last:
                continue
            if step == 0:
                start_group(g)
            elif step <= levels:
                if g == 0:
                    if step + 1 < levels:
                        advance_block(step + 1)
                    if step < levels:
                        advance_gram(step)
                    if step == 1:
                        share_gram(0)
                up(g, step - 1)
                if g == 0 and step < levels:
                    share_gram(step)
                if step == levels:
                    share_early(g)
            elif step == levels + 1:
                share_late(g)
            else:
                end_group(g)

    for copy in sent:
        copy.wait_send()
    for copy in finals:
        copy.wait()


def move_kernel(pieces, source, out, held, in_sem, out_sem):
    step = source.shape[0] // pieces
    places = [pl.ds(i * step, step) for i in range(pieces)]
    arrive = [
        pltpu.make_async_copy(source.at[p], held.at[p], in_sem.at[i]) for i, p in enumerate(places)
    ]
    leave = [pltpu.make_async_copy(held.at[p], out.at[p], out_sem.at[i]) for i, p in enumerate(places)]
    for copy in arrive:
        copy.start()
    for first, second in zip(arrive, leave):
        first.wait()
        second.start()
    for copy in leave:
        copy.wait()


def body(
    bits_inner,
    levels,
    observed,
    leaf_order,
    leaf_inverse,
    project_basis,
    correct_basis,
    coupling,
    trend_basis,
    trend_correct,
):
    leaf, cols = observed.shape
    wide = correct_basis.shape[1]
    rank = wide // levels
    trend_rank = trend_basis.shape[1]
    group = 256 if cols % 256 == 0 else cols
    groups = cols // group
    held, part, rows, width = plan(group, levels, rank, trend_rank)
    tile = 512 if leaf % 512 == 0 else leaf
    vm = pltpu.VMEM
    every = range(levels)
    scratch = [
        vm((leaf, cols), F32),
        vm((leaf, cols), BF),
        vm(leaf_order.shape, jnp.int32),
        vm((leaf, leaf), BF),
        vm((leaf, wide + trend_rank), BF),
        vm((leaf, wide), BF),
        vm((leaf, trend_rank), BF),
        vm((leaf, leaf), BF),
        vm((leaf, 128), F32),
        vm((leaf, group), BF),
        vm((leaf, cols), F32),
        vm((cols, leaf), BF),
        vm((levels + 1,) + coupling.shape, BF),
        vm((cols, wide + trend_rank), BF),
        vm((2, rank // 2, max(width[0] - rows[1], rank)), BF),
    ]
    for _ in range(groups):
        scratch += [vm((held[0], rows[0]), F32)]
        scratch += [vm((part[s], rows[s + 1]), F32) for s in every]
    scratch += [vm((part[s], rows[s]), BF) for s in every] * (2 * groups)
    scratch += [vm((part[s], rank), BF) for s in every] * groups
    scratch += [vm((2, rank, rows[s + 1]), BF) for s in every]
    scratch += [vm((rank // 2, width[s + 1]), BF) for s in range(levels - 1)] * 2
    late = sum(held[s] != part[s] for s in every)
    reach = (1 << late >> 1) - 1
    copies = 6 * levels + groups * (levels + 2 * reach + reach + 3)
    scratch += [
        pltpu.SemaphoreType.DMA((8 + groups,)),
        pltpu.SemaphoreType.DMA((copies,)),
        pltpu.SemaphoreType.DMA((copies,)),
    ]
    swept = pl.pallas_call(
        functools.partial(sweep_kernel, bits_inner, levels, rank, group, tile),
        out_shape=jax.ShapeDtypeStruct((leaf, cols), F32),
        in_specs=[pl.BlockSpec(memory_space=pltpu.HBM)] * 8,
        out_specs=pl.BlockSpec(memory_space=pl.ANY),
        scratch_shapes=scratch,
        compiler_params=pltpu.CompilerParams(
            collective_id=0, has_side_effects=True, vmem_limit_bytes=56 * 1024 * 1024
        ),
        name="tree_sweep",
    )(
        observed,
        leaf_order,
        leaf_inverse,
        project_basis,
        correct_basis,
        coupling,
        trend_basis,
        trend_correct,
    )
    pieces = 8 if leaf % 64 == 0 else 1
    return pl.pallas_call(
        functools.partial(move_kernel, pieces),
        out_shape=jax.ShapeDtypeStruct((leaf, cols), F32),
        in_specs=[pl.BlockSpec(memory_space=pl.ANY)],
        out_specs=pl.BlockSpec(memory_space=pl.ANY),
        scratch_shapes=[
            vm((leaf, cols), F32),
            pltpu.SemaphoreType.DMA((pieces,)),
            pltpu.SemaphoreType.DMA((pieces,)),
        ],
        compiler_params=pltpu.CompilerParams(vmem_limit_bytes=62 * 1024 * 1024),
        name="move_result",
    )(swept)


def solution(mesh):
    bits_inner = mesh.shape["inner"].bit_length() - 1
    bits_outer = mesh.shape["outer"].bit_length() - 1
    rows = P(("outer", "inner"), None)
    return jax.shard_map(
        functools.partial(body, bits_inner, bits_inner + bits_outer),
        mesh=mesh,
        in_specs=(rows,) * 8,
        out_specs=rows,
        check_vma=False,
    )
```

```python
import functools

import jax
import jax.numpy as jnp
from jax import lax
from jax.experimental import pallas as pl
from jax.experimental.pallas import tpu as pltpu
from jax.sharding import PartitionSpec as P

MESH = pl.DeviceIdType.MESH
BF = jnp.bfloat16
F32 = jnp.float32
NT = (((1,), (1,)), ((), ()))


def dot(a, b):
    return jnp.dot(a, b, preferred_element_type=F32)


def dot_nt(a, b):
    return lax.dot_general(a, b, NT, preferred_element_type=F32)


def plan(cols, levels, rank, trend):
    held, part = [], []
    now = cols
    for _ in range(levels):
        held.append(now)
        if now % 32 == 0:
            now //= 2
        part.append(now)
    rows = [(levels - s) * rank + trend for s in range(levels + 1)]
    width = [sum(rows[s + 1 :]) for s in range(levels)]
    return held, part, rows, width


def sweep_kernel(
    bits_inner,
    levels,
    rank,
    group,
    tile,
    observed,
    order,
    inverse,
    project,
    correct,
    coupling,
    trend,
    trend_correct,
    out,
    obs_v,
    obs_bf,
    order_v,
    inv_v,
    basis_v,
    correct_v,
    trend_v,
    hot_v,
    column_v,
    ordered_v,
    est_v,
    est_t,
    blocks,
    factors,
    gram_local,
    *rest,
):
    leaf, cols = observed.shape
    trend_rank = trend.shape[1]
    groups = cols // group
    held, part, rows, width = plan(group, levels, rank, trend_rank)
    rest = list(rest)

    def take(n):
        taken = rest[:n]
        del rest[:n]
        return taken

    sums = [take(levels + 1) for _ in range(groups)]
    x_send = [take(levels) for _ in range(groups)]
    x_recv = [take(levels) for _ in range(groups)]
    sib = [take(levels) for _ in range(groups)]
    gram = take(levels)
    gram_rest = take(levels - 1)
    gram_in = take(levels - 1)
    local_sem, send_sem, recv_sem = rest

    outer, inner = lax.axis_index("outer"), lax.axis_index("inner")
    bits, partners = [], []
    for s in range(levels):
        if s < bits_inner:
            span = 1 << s
            bit = lax.rem(inner // span, 2)
            partners.append((outer, inner + (1 - 2 * bit) * span))
        else:
            span = 1 << (s - bits_inner)
            bit = lax.rem(outer // span, 2)
            partners.append((outer + (1 - 2 * bit) * span, inner))
        bits.append(bit)
    side = bits[0]
    split = [s for s in range(levels) if held[s] != part[s]]
    late = len(split)

    def across(mask):
        to_outer, to_inner = outer, inner
        for s in range(levels):
            if mask >> s & 1:
                if s < bits_inner:
                    to_inner = to_inner + (1 - 2 * bits[s]) * (1 << s)
                else:
                    to_outer = to_outer + (1 - 2 * bits[s]) * (1 << (s - bits_inner))
        return to_outer, to_inner

    wide_masks = [m for m in range(2, 1 << late, 2)]
    partners = {1 << s: partners[s] for s in range(levels)}
    for mask in wide_masks:
        partners.setdefault(mask, across(mask))

    def local(src, dst, i):
        copy = pltpu.make_async_copy(src, dst, local_sem.at[i])
        copy.start()
        return copy

    wide = levels * rank
    c_block = local(coupling, blocks.at[0], 0)
    c_correct = local(correct, correct_v, 1)
    c_project = local(project, basis_v.at[:, pl.ds(0, wide)], 2)
    c_trend = local(trend, basis_v.at[:, pl.ds(wide, trend_rank)], 3)
    c_order = local(order, order_v, 4)

    barrier = pltpu.get_barrier_semaphore()
    for partner in partners.values():
        pl.semaphore_signal(barrier, inc=1, device_id=partner, device_id_type=MESH)
    pl.semaphore_wait(barrier, len(partners))

    sent = []

    def remote(src, dst, mask):
        slot = len(sent)
        copy = pltpu.make_async_remote_copy(
            src_ref=src,
            dst_ref=dst,
            send_sem=send_sem.at[slot],
            recv_sem=recv_sem.at[slot],
            device_id=partners[mask],
            device_id_type=MESH,
        )
        copy.start()
        sent.append(copy)
        return copy

    block_rows = coupling.shape[0] // 2
    gram_rows = rank // 2
    my_block = pl.ds(pl.multiple_of(side * block_rows, block_rows), block_rows)
    my_gram = pl.ds(pl.multiple_of(side * gram_rows, gram_rows), gram_rows)
    move = {}
    pending = jnp.int32(0)
    block_of = []

    def send_block(s):
        if s == 0:
            move["block", s] = remote(blocks.at[0], blocks.at[1], 1)
        else:
            place = blocks.at[s + 1, my_block]
            move["block", s] = remote(blocks.at[pending, my_block], place, 1 << s)

    def send_gram(s):
        if s == 0:
            if levels > 1:
                move["rest", s] = remote(gram_local.at[1 - side], gram_in[0], 1)
            move["gram", s] = remote(gram[0].at[0], gram[0].at[1], 1)
            return
        if s + 1 < levels:
            move["rest", s] = remote(gram_rest[s], gram_in[s], 1 << s)
        mine = gram[s].at[0, my_gram]
        move["gram", s] = remote(mine, gram[s].at[1, my_gram], 1 << s)
        move["own", s] = remote(mine, mine, 1)

    def advance_block(s):
        nonlocal pending
        move["block", s].wait_recv()
        block_of.append(jnp.where(bits[s] == 1, pending, s + 1))
        pending = jnp.where(bits[s] == 1, s + 1, pending)
        if s + 1 < levels:
            send_block(s + 1)
        if s > 0:
            block = blocks.at[s + 1, my_block]
            move["block2", s] = remote(block, block, 1)

    def advance_gram(s):
        if s + 1 >= levels:
            return
        move["rest", s].wait_recv()
        here = gram_local[side] if s == 0 else gram_rest[s][...]
        total = (here.astype(F32) + gram_in[s][...].astype(F32)).astype(BF)
        skip = rows[s + 2]
        if s + 2 < levels:
            gram_rest[s + 1][...] = total[:, skip:]
        gram[s + 1][0, my_gram, :] = total[:, :skip]
        send_gram(s + 1)

    def share_gram(s):
        move["gram", s].wait_recv()
        if s > 0:
            other = gram[s].at[1, my_gram]
            move["other", s] = remote(other, other, 1)

    def ready(s):
        if s > 0:
            move["block2", s].wait_recv()
            move["own", s].wait_recv()
            move["other", s].wait_recv()

    c_block.wait()
    send_block(0)

    c_correct.wait()
    c_project.wait()
    c_trend.wait()
    c_inv = local(inverse, inv_v, 5)
    c_obs = local(observed, obs_v, 6)
    c_last = local(trend_correct, trend_v, 7)
    at = 0
    for s in range(0, levels, 2):
        both = min(2, levels - s)
        columns_t = correct_v[:, s * rank : (s + both) * rank].T
        pair = dot(columns_t, basis_v[:, (s + 1) * rank :]).astype(BF)
        for u in range(both):
            value = pair[u * rank : (u + 1) * rank, u * rank :]
            if s + u == 0:
                gram[0][0] = value
            else:
                gram_local[0, :, at : at + rows[s + u + 1]] = value[:gram_rows]
                gram_local[1, :, at : at + rows[s + u + 1]] = value[gram_rows:]
                at += rows[s + u + 1]
    send_gram(0)
    advance_block(0)

    c_order.wait()
    steps = leaf // tile
    column_v[...] = jnp.broadcast_to(order_v[...].astype(F32), (128, leaf)).T
    blocks_wide = leaf // 128

    def make_hot(t, carry):
        place = pl.ds(pl.multiple_of(t * 128, 128), 128)
        column = column_v[place, :]
        lane = lax.broadcasted_iota(jnp.int32, (128, 128), 1).astype(F32)
        for k in range(blocks_wide):
            hit = column == lane + float(128 * k)
            hot_v[place, k * 128 : (k + 1) * 128] = jnp.where(hit, 1.0, 0.0).astype(BF)
        return carry

    lax.fori_loop(0, blocks_wide, make_hot, 0)
    advance_gram(0)
    c_inv.wait()

    if levels > 1:
        advance_block(1)
    c_obs.wait()
    c_last.wait()

    x_move, early, late_move, core_move = {}, {}, {}, {}
    offsets = [[jnp.int32(g * group)] for g in range(groups)]
    finals = []

    def send_x(g, s):
        x_move[g, s] = remote(x_send[g][s], x_recv[g][s], 1 << s)

    def start_group(g):
        lanes = slice(g * group, (g + 1) * group)

        def make_ordered(t, carry):
            r0 = pl.multiple_of(t * tile, tile)
            value = dot(hot_v[pl.ds(r0, tile), :], obs_bf[:, lanes])
            ordered_v[pl.ds(r0, tile), :] = value.astype(BF)
            return carry

        def make_estimate(t, carry):
            r0 = pl.multiple_of(t * tile, tile)
            value = dot(inv_v[pl.ds(r0, tile), :], ordered_v[...])
            est_v[pl.ds(r0, tile), lanes] = value
            est_t[lanes, pl.ds(r0, tile)] = value.astype(BF).T
            return carry

        obs_bf[:, lanes] = obs_v[:, lanes].astype(BF)
        lax.fori_loop(0, steps, make_ordered, 0)
        lax.fori_loop(0, steps, make_estimate, 0)
        sums[g][0][...] = dot(est_t[lanes, :], basis_v[...])
        if held[0] != part[0]:
            away = pl.ds(pl.multiple_of((1 - side) * part[0], part[0]), part[0])
            x_send[g][0][...] = sums[g][0][away, :].astype(BF)
        else:
            x_send[g][0][...] = sums[g][0][...].astype(BF)
        send_x(g, 0)

    def up(g, s):
        count = part[s]
        halves = held[s] != part[s]
        first_side = bits[s] == 0
        offset = offsets[g][s] + (bits[s] * count if halves else 0)
        offset = pl.multiple_of(offset, count)
        offsets[g].append(offset)
        if not halves:
            own = sums[g][s][...]
        else:
            own = sums[g][s][pl.ds(pl.multiple_of(bits[s] * count, count), count), :]
        x_move[g, s].wait_recv()
        if g == 0:
            ready(s)
        other = x_recv[g][s][...].astype(F32)
        own_head, other_head = own[:, :rank], other[:, :rank]
        one = jnp.where(first_side, own_head, other_head).astype(BF)
        two = jnp.where(first_side, other_head, own_head).astype(BF)
        stacked = jnp.concatenate([one, two], 1)
        factor = dot_nt(stacked, blocks[block_of[s]])
        mine = jnp.where(first_side, factor[:, :rank], factor[:, rank:]).astype(BF)
        theirs = jnp.where(first_side, factor[:, rank:], factor[:, :rank]).astype(BF)
        new = (
            own[:, rank:]
            + other[:, rank:]
            - dot(jnp.concatenate([mine, theirs], 1), gram[s][...].reshape(2 * rank, rows[s + 1]))
        )
        sums[g][s + 1][...] = new
        if s + 1 < levels:
            after = part[s + 1]
            if held[s + 1] != after:
                away = pl.multiple_of((1 - bits[s + 1]) * after, after)
                x_send[g][s + 1][...] = sums[g][s + 1][pl.ds(away, after), :].astype(BF)
            else:
                x_send[g][s + 1][...] = new.astype(BF)
            send_x(g, s + 1)
        factors[pl.ds(offset, count), s * rank : (s + 1) * rank] = mine
        if halves:
            sib[g][s][...] = theirs
        if s + 1 == levels:
            trend_factor = dot_nt(new.astype(BF), blocks[pending]).astype(BF)
            factors[pl.ds(offset, count), wide:] = trend_factor
            place = factors.at[pl.ds(offset, count), pl.ds(late * rank, rows[late])]
            for mask in wide_masks:
                late_move[g, mask] = remote(place, place, mask)
        if halves:
            place = factors.at[pl.ds(offset, count), pl.ds(s * rank, rank)]
            masks = [1] if s == 0 else [m for m in wide_masks if m < 2 << s]
            for mask in masks:
                source = sib[g][s] if mask >> s & 1 else place
                early[g, s, mask] = remote(source, place, mask)

    def core_rows(g):
        return pl.ds(pl.multiple_of(g * group + side * part[0], part[0]), part[0])

    def share_early(g):
        for s in split[1:]:
            for mask in wide_masks:
                if (g, s, mask) in early:
                    early[g, s, mask].wait_recv()
        if late > 1:
            place = factors.at[core_rows(g), pl.ds(rank, (late - 1) * rank)]
            core_move[g, 0] = remote(place, place, 1)

    def share_late(g):
        for mask in wide_masks:
            late_move[g, mask].wait_recv()
        place = factors.at[core_rows(g), pl.ds(late * rank, rows[late])]
        core_move[g, 1] = remote(place, place, 1)

    def end_group(g):
        early[g, 0, 1].wait_recv()
        if late > 1:
            core_move[g, 0].wait_recv()
        core_move[g, 1].wait_recv()
        finish(g)

    def finish(g):
        lanes = slice(g * group, (g + 1) * group)

        def apply(t, carry):
            r0 = pl.multiple_of(t * tile, tile)
            place = pl.ds(r0, tile)
            est_v[place, lanes] = (
                est_v[place, lanes]
                - dot_nt(correct_v[place, :], factors[lanes, :wide])
                - dot_nt(trend_v[place, :], factors[lanes, wide:])
            )
            return carry

        lax.fori_loop(0, steps, apply, 0)
        mine = pl.ds(g * group, group)
        finals.append(local(est_v.at[:, mine], out.at[:, mine], 8 + g))

    last = 3 + levels
    for wave in range(last + groups - 1):
        for g in reversed(range(groups)):
            step = wave - g
            if step < 0 or step >= last:
                continue
            if step == 0:
                start_group(g)
            elif step <= levels:
                if g == 0:
                    if step + 1 < levels:
                        advance_block(step + 1)
                    if step < levels:
                        advance_gram(step)
                    if step == 1:
                        share_gram(0)
                up(g, step - 1)
                if g == 0 and step < levels:
                    share_gram(step)
                if step == levels:
                    share_early(g)
            elif step == levels + 1:
                share_late(g)
            else:
                end_group(g)

    for copy in sent:
        copy.wait_send()
    for copy in finals:
        copy.wait()


def move_kernel(pieces, source, out, held, in_sem, out_sem):
    step = source.shape[0] // pieces
    places = [pl.ds(i * step, step) for i in range(pieces)]
    arrive = [
        pltpu.make_async_copy(source.at[p], held.at[p], in_sem.at[i]) for i, p in enumerate(places)
    ]
    leave = [pltpu.make_async_copy(held.at[p], out.at[p], out_sem.at[i]) for i, p in enumerate(places)]
    for copy in arrive:
        copy.start()
    for first, second in zip(arrive, leave):
        first.wait()
        second.start()
    for copy in leave:
        copy.wait()


def body(
    bits_inner,
    levels,
    observed,
    leaf_order,
    leaf_inverse,
    project_basis,
    correct_basis,
    coupling,
    trend_basis,
    trend_correct,
):
    leaf, cols = observed.shape
    wide = correct_basis.shape[1]
    rank = wide // levels
    trend_rank = trend_basis.shape[1]
    group = 256 if cols % 256 == 0 else cols
    groups = cols // group
    held, part, rows, width = plan(group, levels, rank, trend_rank)
    tile = 512 if leaf % 512 == 0 else leaf
    vm = pltpu.VMEM
    every = range(levels)
    scratch = [
        vm((leaf, cols), F32),
        vm((leaf, cols), BF),
        vm(leaf_order.shape, jnp.int32),
        vm((leaf, leaf), BF),
        vm((leaf, wide + trend_rank), BF),
        vm((leaf, wide), BF),
        vm((leaf, trend_rank), BF),
        vm((leaf, leaf), BF),
        vm((leaf, 128), F32),
        vm((leaf, group), BF),
        vm((leaf, cols), F32),
        vm((cols, leaf), BF),
        vm((levels + 1,) + coupling.shape, BF),
        vm((cols, wide + trend_rank), BF),
        vm((2, rank // 2, max(width[0] - rows[1], rank)), BF),
    ]
    for _ in range(groups):
        scratch += [vm((held[0], rows[0]), F32)]
        scratch += [vm((part[s], rows[s + 1]), F32) for s in every]
    scratch += [vm((part[s], rows[s]), BF) for s in every] * (2 * groups)
    scratch += [vm((part[s], rank), BF) for s in every] * groups
    scratch += [vm((2, rank, rows[s + 1]), BF) for s in every]
    scratch += [vm((rank // 2, width[s + 1]), BF) for s in range(levels - 1)] * 2
    late = sum(held[s] != part[s] for s in every)
    reach = (1 << late >> 1) - 1
    copies = 6 * levels + groups * (levels + 2 * reach + reach + 3)
    scratch += [
        pltpu.SemaphoreType.DMA((8 + groups,)),
        pltpu.SemaphoreType.DMA((copies,)),
        pltpu.SemaphoreType.DMA((copies,)),
    ]
    swept = pl.pallas_call(
        functools.partial(sweep_kernel, bits_inner, levels, rank, group, tile),
        out_shape=jax.ShapeDtypeStruct((leaf, cols), F32),
        in_specs=[pl.BlockSpec(memory_space=pltpu.HBM)] * 8,
        out_specs=pl.BlockSpec(memory_space=pl.ANY),
        scratch_shapes=scratch,
        compiler_params=pltpu.CompilerParams(
            collective_id=0, has_side_effects=True, vmem_limit_bytes=56 * 1024 * 1024
        ),
        name="tree_sweep",
    )(
        observed,
        leaf_order,
        leaf_inverse,
        project_basis,
        correct_basis,
        coupling,
        trend_basis,
        trend_correct,
    )
    pieces = 8 if leaf % 64 == 0 else 1
    return pl.pallas_call(
        functools.partial(move_kernel, pieces),
        out_shape=jax.ShapeDtypeStruct((leaf, cols), F32),
        in_specs=[pl.BlockSpec(memory_space=pl.ANY)],
        out_specs=pl.BlockSpec(memory_space=pl.ANY),
        scratch_shapes=[
            vm((leaf, cols), F32),
            pltpu.SemaphoreType.DMA((pieces,)),
            pltpu.SemaphoreType.DMA((pieces,)),
        ],
        compiler_params=pltpu.CompilerParams(vmem_limit_bytes=62 * 1024 * 1024),
        name="move_result",
    )(swept)


def solution(mesh):
    bits_inner = mesh.shape["inner"].bit_length() - 1
    bits_outer = mesh.shape["outer"].bit_length() - 1
    rows = P(("outer", "inner"), None)
    return jax.shard_map(
        functools.partial(body, bits_inner, bits_inner + bits_outer),
        mesh=mesh,
        in_specs=(rows,) * 8,
        out_specs=rows,
        check_vma=False,
    )
```

```python
import functools

import jax
import jax.numpy as jnp
from jax import lax
from jax.experimental import pallas as pl
from jax.experimental.pallas import tpu as pltpu
from jax.sharding import PartitionSpec as P

MESH = pl.DeviceIdType.MESH
BF = jnp.bfloat16
F32 = jnp.float32
NT = (((1,), (1,)), ((), ()))


def dot(a, b):
    return jnp.dot(a, b, preferred_element_type=F32)


def dot_nt(a, b):
    return lax.dot_general(a, b, NT, preferred_element_type=F32)


def plan(cols, levels, rank, trend):
    held, part = [], []
    now = cols
    for _ in range(levels):
        held.append(now)
        if now % 32 == 0:
            now //= 2
        part.append(now)
    rows = [(levels - s) * rank + trend for s in range(levels + 1)]
    width = [sum(rows[s + 1 :]) for s in range(levels)]
    return held, part, rows, width


def sweep_kernel(
    bits_inner,
    levels,
    rank,
    group,
    tile,
    observed,
    order,
    inverse,
    project,
    correct,
    coupling,
    trend,
    trend_correct,
    out,
    obs_v,
    obs_bf,
    order_v,
    inv_v,
    basis_v,
    correct_v,
    trend_v,
    hot_v,
    column_v,
    ordered_v,
    est_v,
    est_t,
    blocks,
    factors,
    gram_local,
    *rest,
):
    leaf, cols = observed.shape
    trend_rank = trend.shape[1]
    groups = cols // group
    held, part, rows, width = plan(group, levels, rank, trend_rank)
    rest = list(rest)

    def take(n):
        taken = rest[:n]
        del rest[:n]
        return taken

    sums = [take(levels + 1) for _ in range(groups)]
    x_send = [take(levels) for _ in range(groups)]
    x_recv = [take(levels) for _ in range(groups)]
    sib = [take(levels) for _ in range(groups)]
    gram = take(levels)
    gram_rest = take(levels - 1)
    gram_in = take(levels - 1)
    local_sem, send_sem, recv_sem = rest

    outer, inner = lax.axis_index("outer"), lax.axis_index("inner")
    bits, partners = [], []
    for s in range(levels):
        if s < bits_inner:
            span = 1 << s
            bit = lax.rem(inner // span, 2)
            partners.append((outer, inner + (1 - 2 * bit) * span))
        else:
            span = 1 << (s - bits_inner)
            bit = lax.rem(outer // span, 2)
            partners.append((outer + (1 - 2 * bit) * span, inner))
        bits.append(bit)
    side = bits[0]
    split = [s for s in range(levels) if held[s] != part[s]]
    late = len(split)

    def across(mask):
        to_outer, to_inner = outer, inner
        for s in range(levels):
            if mask >> s & 1:
                if s < bits_inner:
                    to_inner = to_inner + (1 - 2 * bits[s]) * (1 << s)
                else:
                    to_outer = to_outer + (1 - 2 * bits[s]) * (1 << (s - bits_inner))
        return to_outer, to_inner

    wide_masks = [m for m in range(2, 1 << late, 2)]
    partners = {1 << s: partners[s] for s in range(levels)}
    for mask in wide_masks:
        partners.setdefault(mask, across(mask))

    def local(src, dst, i):
        copy = pltpu.make_async_copy(src, dst, local_sem.at[i])
        copy.start()
        return copy

    wide = levels * rank
    c_block = local(coupling, blocks.at[0], 0)
    c_correct = local(correct, correct_v, 1)
    c_project = local(project, basis_v.at[:, pl.ds(0, wide)], 2)
    c_trend = local(trend, basis_v.at[:, pl.ds(wide, trend_rank)], 3)
    c_order = local(order, order_v, 4)

    barrier = pltpu.get_barrier_semaphore()
    for partner in partners.values():
        pl.semaphore_signal(barrier, inc=1, device_id=partner, device_id_type=MESH)
    pl.semaphore_wait(barrier, len(partners))

    sent = []

    def remote(src, dst, mask):
        slot = len(sent)
        copy = pltpu.make_async_remote_copy(
            src_ref=src,
            dst_ref=dst,
            send_sem=send_sem.at[slot],
            recv_sem=recv_sem.at[slot],
            device_id=partners[mask],
            device_id_type=MESH,
        )
        copy.start()
        sent.append(copy)
        return copy

    block_rows = coupling.shape[0] // 2
    gram_rows = rank // 2
    my_block = pl.ds(pl.multiple_of(side * block_rows, block_rows), block_rows)
    my_gram = pl.ds(pl.multiple_of(side * gram_rows, gram_rows), gram_rows)
    move = {}
    pending = jnp.int32(0)
    block_of = []

    def send_block(s):
        if s == 0:
            move["block", s] = remote(blocks.at[0], blocks.at[1], 1)
        else:
            place = blocks.at[s + 1, my_block]
            move["block", s] = remote(blocks.at[pending, my_block], place, 1 << s)

    def send_gram(s):
        if s == 0:
            if levels > 1:
                move["rest", s] = remote(gram_local.at[1 - side], gram_in[0], 1)
            move["gram", s] = remote(gram[0].at[0], gram[0].at[1], 1)
            return
        if s + 1 < levels:
            move["rest", s] = remote(gram_rest[s], gram_in[s], 1 << s)
        mine = gram[s].at[0, my_gram]
        move["gram", s] = remote(mine, gram[s].at[1, my_gram], 1 << s)
        move["own", s] = remote(mine, mine, 1)

    def advance_block(s):
        nonlocal pending
        move["block", s].wait_recv()
        block_of.append(jnp.where(bits[s] == 1, pending, s + 1))
        pending = jnp.where(bits[s] == 1, s + 1, pending)
        if s + 1 < levels:
            send_block(s + 1)
        if s > 0:
            block = blocks.at[s + 1, my_block]
            move["block2", s] = remote(block, block, 1)

    def advance_gram(s):
        if s + 1 >= levels:
            return
        move["rest", s].wait_recv()
        here = gram_local[side] if s == 0 else gram_rest[s][...]
        total = (here.astype(F32) + gram_in[s][...].astype(F32)).astype(BF)
        skip = rows[s + 2]
        if s + 2 < levels:
            gram_rest[s + 1][...] = total[:, skip:]
        gram[s + 1][0, my_gram, :] = total[:, :skip]
        send_gram(s + 1)

    def share_gram(s):
        move["gram", s].wait_recv()
        if s > 0:
            other = gram[s].at[1, my_gram]
            move["other", s] = remote(other, other, 1)

    def ready(s):
        if s > 0:
            move["block2", s].wait_recv()
            move["own", s].wait_recv()
            move["other", s].wait_recv()

    c_block.wait()
    send_block(0)

    c_correct.wait()
    c_project.wait()
    c_trend.wait()
    c_inv = local(inverse, inv_v, 5)
    c_obs = local(observed, obs_v, 6)
    c_last = local(trend_correct, trend_v, 7)
    at = 0
    for s in range(0, levels, 2):
        both = min(2, levels - s)
        columns_t = correct_v[:, s * rank : (s + both) * rank].T
        pair = dot(columns_t, basis_v[:, (s + 1) * rank :]).astype(BF)
        for u in range(both):
            value = pair[u * rank : (u + 1) * rank, u * rank :]
            if s + u == 0:
                gram[0][0] = value
            else:
                gram_local[0, :, at : at + rows[s + u + 1]] = value[:gram_rows]
                gram_local[1, :, at : at + rows[s + u + 1]] = value[gram_rows:]
                at += rows[s + u + 1]
    send_gram(0)
    advance_block(0)

    c_order.wait()
    steps = leaf // tile
    column_v[...] = jnp.broadcast_to(order_v[...].astype(F32), (128, leaf)).T
    blocks_wide = leaf // 128

    def make_hot(t, carry):
        place = pl.ds(pl.multiple_of(t * 128, 128), 128)
        column = column_v[place, :]
        lane = lax.broadcasted_iota(jnp.int32, (128, 128), 1).astype(F32)
        for k in range(blocks_wide):
            hit = column == lane + float(128 * k)
            hot_v[place, k * 128 : (k + 1) * 128] = jnp.where(hit, 1.0, 0.0).astype(BF)
        return carry

    lax.fori_loop(0, blocks_wide, make_hot, 0)
    advance_gram(0)
    c_inv.wait()

    if levels > 1:
        advance_block(1)
    c_obs.wait()
    c_last.wait()

    x_move, early, late_move, core_move = {}, {}, {}, {}
    offsets = [[jnp.int32(g * group)] for g in range(groups)]
    finals = []

    def send_x(g, s):
        x_move[g, s] = remote(x_send[g][s], x_recv[g][s], 1 << s)

    def start_group(g):
        lanes = slice(g * group, (g + 1) * group)

        def make_ordered(t, carry):
            r0 = pl.multiple_of(t * tile, tile)
            value = dot(hot_v[pl.ds(r0, tile), :], obs_bf[:, lanes])
            ordered_v[pl.ds(r0, tile), :] = value.astype(BF)
            return carry

        def make_estimate(t, carry):
            r0 = pl.multiple_of(t * tile, tile)
            value = dot(inv_v[pl.ds(r0, tile), :], ordered_v[...])
            est_v[pl.ds(r0, tile), lanes] = value
            est_t[lanes, pl.ds(r0, tile)] = value.astype(BF).T
            return carry

        obs_bf[:, lanes] = obs_v[:, lanes].astype(BF)
        lax.fori_loop(0, steps, make_ordered, 0)
        lax.fori_loop(0, steps, make_estimate, 0)
        sums[g][0][...] = dot(est_t[lanes, :], basis_v[...])
        if held[0] != part[0]:
            away = pl.ds(pl.multiple_of((1 - side) * part[0], part[0]), part[0])
            x_send[g][0][...] = sums[g][0][away, :].astype(BF)
        else:
            x_send[g][0][...] = sums[g][0][...].astype(BF)
        send_x(g, 0)

    def up(g, s):
        count = part[s]
        halves = held[s] != part[s]
        first_side = bits[s] == 0
        offset = offsets[g][s] + (bits[s] * count if halves else 0)
        offset = pl.multiple_of(offset, count)
        offsets[g].append(offset)
        if not halves:
            own = sums[g][s][...]
        else:
            own = sums[g][s][pl.ds(pl.multiple_of(bits[s] * count, count), count), :]
        x_move[g, s].wait_recv()
        if g == 0:
            ready(s)
        other = x_recv[g][s][...].astype(F32)
        own_head, other_head = own[:, :rank], other[:, :rank]
        one = jnp.where(first_side, own_head, other_head).astype(BF)
        two = jnp.where(first_side, other_head, own_head).astype(BF)
        stacked = jnp.concatenate([one, two], 1)
        factor = dot_nt(stacked, blocks[block_of[s]])
        mine = jnp.where(first_side, factor[:, :rank], factor[:, rank:]).astype(BF)
        theirs = jnp.where(first_side, factor[:, rank:], factor[:, :rank]).astype(BF)
        new = (
            own[:, rank:]
            + other[:, rank:]
            - dot(jnp.concatenate([mine, theirs], 1), gram[s][...].reshape(2 * rank, rows[s + 1]))
        )
        sums[g][s + 1][...] = new
        if s + 1 < levels:
            after = part[s + 1]
            if held[s + 1] != after:
                away = pl.multiple_of((1 - bits[s + 1]) * after, after)
                x_send[g][s + 1][...] = sums[g][s + 1][pl.ds(away, after), :].astype(BF)
            else:
                x_send[g][s + 1][...] = new.astype(BF)
            send_x(g, s + 1)
        factors[pl.ds(offset, count), s * rank : (s + 1) * rank] = mine
        if halves:
            sib[g][s][...] = theirs
        if s + 1 == levels:
            trend_factor = dot_nt(new.astype(BF), blocks[pending]).astype(BF)
            factors[pl.ds(offset, count), wide:] = trend_factor
            place = factors.at[pl.ds(offset, count), pl.ds(late * rank, rows[late])]
            for mask in wide_masks:
                late_move[g, mask] = remote(place, place, mask)
        if halves:
            place = factors.at[pl.ds(offset, count), pl.ds(s * rank, rank)]
            masks = [1] if s == 0 else [m for m in wide_masks if m < 2 << s]
            for mask in masks:
                source = sib[g][s] if mask >> s & 1 else place
                early[g, s, mask] = remote(source, place, mask)

    def core_rows(g):
        return pl.ds(pl.multiple_of(g * group + side * part[0], part[0]), part[0])

    def share_early(g):
        for s in split[1:]:
            for mask in wide_masks:
                if (g, s, mask) in early:
                    early[g, s, mask].wait_recv()
        if late > 1:
            place = factors.at[core_rows(g), pl.ds(rank, (late - 1) * rank)]
            core_move[g, 0] = remote(place, place, 1)

    def share_late(g):
        for mask in wide_masks:
            late_move[g, mask].wait_recv()
        place = factors.at[core_rows(g), pl.ds(late * rank, rows[late])]
        core_move[g, 1] = remote(place, place, 1)

    def end_group(g):
        early[g, 0, 1].wait_recv()
        if late > 1:
            core_move[g, 0].wait_recv()
        core_move[g, 1].wait_recv()
        finish(g)

    def finish(g):
        lanes = slice(g * group, (g + 1) * group)

        def apply(t, carry):
            r0 = pl.multiple_of(t * tile, tile)
            place = pl.ds(r0, tile)
            est_v[place, lanes] = (
                est_v[place, lanes]
                - dot_nt(correct_v[place, :], factors[lanes, :wide])
                - dot_nt(trend_v[place, :], factors[lanes, wide:])
            )
            return carry

        lax.fori_loop(0, steps, apply, 0)
        mine = pl.ds(g * group, group)
        finals.append(local(est_v.at[:, mine], out.at[:, mine], 8 + g))

    last = 3 + levels
    for wave in range(last + groups - 1):
        for g in reversed(range(groups)):
            step = wave - g
            if step < 0 or step >= last:
                continue
            if step == 0:
                start_group(g)
            elif step <= levels:
                if g == 0 and step == 1:
                    share_gram(0)
                up(g, step - 1)
                if g == 0 and step < levels:
                    if step + 1 < levels:
                        advance_block(step + 1)
                    advance_gram(step)
                    share_gram(step)
                if step == levels:
                    share_early(g)
            elif step == levels + 1:
                share_late(g)
            else:
                end_group(g)

    for copy in sent:
        copy.wait_send()
    for copy in finals:
        copy.wait()


def move_kernel(pieces, source, out, held, in_sem, out_sem):
    step = source.shape[0] // pieces
    places = [pl.ds(i * step, step) for i in range(pieces)]
    arrive = [
        pltpu.make_async_copy(source.at[p], held.at[p], in_sem.at[i]) for i, p in enumerate(places)
    ]
    leave = [pltpu.make_async_copy(held.at[p], out.at[p], out_sem.at[i]) for i, p in enumerate(places)]
    for copy in arrive:
        copy.start()
    for first, second in zip(arrive, leave):
        first.wait()
        second.start()
    for copy in leave:
        copy.wait()


def body(
    bits_inner,
    levels,
    observed,
    leaf_order,
    leaf_inverse,
    project_basis,
    correct_basis,
    coupling,
    trend_basis,
    trend_correct,
):
    leaf, cols = observed.shape
    wide = correct_basis.shape[1]
    rank = wide // levels
    trend_rank = trend_basis.shape[1]
    group = 256 if cols % 256 == 0 else cols
    groups = cols // group
    held, part, rows, width = plan(group, levels, rank, trend_rank)
    tile = 512 if leaf % 512 == 0 else leaf
    vm = pltpu.VMEM
    every = range(levels)
    scratch = [
        vm((leaf, cols), F32),
        vm((leaf, cols), BF),
        vm(leaf_order.shape, jnp.int32),
        vm((leaf, leaf), BF),
        vm((leaf, wide + trend_rank), BF),
        vm((leaf, wide), BF),
        vm((leaf, trend_rank), BF),
        vm((leaf, leaf), BF),
        vm((leaf, 128), F32),
        vm((leaf, group), BF),
        vm((leaf, cols), F32),
        vm((cols, leaf), BF),
        vm((levels + 1,) + coupling.shape, BF),
        vm((cols, wide + trend_rank), BF),
        vm((2, rank // 2, max(width[0] - rows[1], rank)), BF),
    ]
    for _ in range(groups):
        scratch += [vm((held[0], rows[0]), F32)]
        scratch += [vm((part[s], rows[s + 1]), F32) for s in every]
    scratch += [vm((part[s], rows[s]), BF) for s in every] * (2 * groups)
    scratch += [vm((part[s], rank), BF) for s in every] * groups
    scratch += [vm((2, rank, rows[s + 1]), BF) for s in every]
    scratch += [vm((rank // 2, width[s + 1]), BF) for s in range(levels - 1)] * 2
    late = sum(held[s] != part[s] for s in every)
    reach = (1 << late >> 1) - 1
    copies = 6 * levels + groups * (levels + 2 * reach + reach + 3)
    scratch += [
        pltpu.SemaphoreType.DMA((8 + groups,)),
        pltpu.SemaphoreType.DMA((copies,)),
        pltpu.SemaphoreType.DMA((copies,)),
    ]
    swept = pl.pallas_call(
        functools.partial(sweep_kernel, bits_inner, levels, rank, group, tile),
        out_shape=jax.ShapeDtypeStruct((leaf, cols), F32),
        in_specs=[pl.BlockSpec(memory_space=pltpu.HBM)] * 8,
        out_specs=pl.BlockSpec(memory_space=pl.ANY),
        scratch_shapes=scratch,
        compiler_params=pltpu.CompilerParams(
            collective_id=0, has_side_effects=True, vmem_limit_bytes=56 * 1024 * 1024
        ),
        name="tree_sweep",
    )(
        observed,
        leaf_order,
        leaf_inverse,
        project_basis,
        correct_basis,
        coupling,
        trend_basis,
        trend_correct,
    )
    pieces = 8 if leaf % 64 == 0 else 1
    return pl.pallas_call(
        functools.partial(move_kernel, pieces),
        out_shape=jax.ShapeDtypeStruct((leaf, cols), F32),
        in_specs=[pl.BlockSpec(memory_space=pl.ANY)],
        out_specs=pl.BlockSpec(memory_space=pl.ANY),
        scratch_shapes=[
            vm((leaf, cols), F32),
            pltpu.SemaphoreType.DMA((pieces,)),
            pltpu.SemaphoreType.DMA((pieces,)),
        ],
        compiler_params=pltpu.CompilerParams(vmem_limit_bytes=62 * 1024 * 1024),
        name="move_result",
    )(swept)


def solution(mesh):
    bits_inner = mesh.shape["inner"].bit_length() - 1
    bits_outer = mesh.shape["outer"].bit_length() - 1
    rows = P(("outer", "inner"), None)
    return jax.shard_map(
        functools.partial(body, bits_inner, bits_inner + bits_outer),
        mesh=mesh,
        in_specs=(rows,) * 8,
        out_specs=rows,
        check_vma=False,
    )
```

```python
import functools

import jax
import jax.numpy as jnp
from jax import lax
from jax.experimental import pallas as pl
from jax.experimental.pallas import tpu as pltpu
from jax.sharding import PartitionSpec as P

MESH = pl.DeviceIdType.MESH
BF = jnp.bfloat16
F32 = jnp.float32
NT = (((1,), (1,)), ((), ()))


def dot(a, b):
    return jnp.dot(a, b, preferred_element_type=F32)


def dot_nt(a, b):
    return lax.dot_general(a, b, NT, preferred_element_type=F32)


def plan(cols, levels, rank, trend):
    held, part = [], []
    now = cols
    for _ in range(levels):
        held.append(now)
        if now % 32 == 0:
            now //= 2
        part.append(now)
    rows = [(levels - s) * rank + trend for s in range(levels + 1)]
    width = [sum(rows[s + 1 :]) for s in range(levels)]
    return held, part, rows, width


def sweep_kernel(
    bits_inner,
    levels,
    rank,
    group,
    tile,
    observed,
    order,
    inverse,
    project,
    correct,
    coupling,
    trend,
    trend_correct,
    out,
    obs_v,
    obs_bf,
    order_v,
    inv_v,
    basis_v,
    correct_v,
    trend_v,
    hot_v,
    column_v,
    ordered_v,
    est_v,
    est_t,
    blocks,
    factors,
    gram_local,
    *rest,
):
    leaf, cols = observed.shape
    trend_rank = trend.shape[1]
    groups = cols // group
    held, part, rows, width = plan(group, levels, rank, trend_rank)
    rest = list(rest)

    def take(n):
        taken = rest[:n]
        del rest[:n]
        return taken

    sums = [take(levels + 1) for _ in range(groups)]
    x_send = [take(levels) for _ in range(groups)]
    x_recv = [take(levels) for _ in range(groups)]
    sib = [take(levels) for _ in range(groups)]
    gram = take(levels)
    gram_rest = take(levels - 1)
    gram_in = take(levels - 1)
    local_sem, send_sem, recv_sem = rest

    outer, inner = lax.axis_index("outer"), lax.axis_index("inner")
    bits, partners = [], []
    for s in range(levels):
        if s < bits_inner:
            span = 1 << s
            bit = lax.rem(inner // span, 2)
            partners.append((outer, inner + (1 - 2 * bit) * span))
        else:
            span = 1 << (s - bits_inner)
            bit = lax.rem(outer // span, 2)
            partners.append((outer + (1 - 2 * bit) * span, inner))
        bits.append(bit)
    side = bits[0]
    split = [s for s in range(levels) if held[s] != part[s]]
    late = len(split)

    def across(mask):
        to_outer, to_inner = outer, inner
        for s in range(levels):
            if mask >> s & 1:
                if s < bits_inner:
                    to_inner = to_inner + (1 - 2 * bits[s]) * (1 << s)
                else:
                    to_outer = to_outer + (1 - 2 * bits[s]) * (1 << (s - bits_inner))
        return to_outer, to_inner

    wide_masks = [m for m in range(2, 1 << late, 2)]
    partners = {1 << s: partners[s] for s in range(levels)}
    for mask in wide_masks:
        partners.setdefault(mask, across(mask))

    def local(src, dst, i):
        copy = pltpu.make_async_copy(src, dst, local_sem.at[i])
        copy.start()
        return copy

    wide = levels * rank
    c_block = local(coupling, blocks.at[0], 0)
    c_correct = local(correct, correct_v, 1)
    c_project = local(project, basis_v.at[:, pl.ds(0, wide)], 2)
    c_trend = local(trend, basis_v.at[:, pl.ds(wide, trend_rank)], 3)
    c_order = local(order, order_v, 4)

    barrier = pltpu.get_barrier_semaphore()
    for partner in partners.values():
        pl.semaphore_signal(barrier, inc=1, device_id=partner, device_id_type=MESH)
    pl.semaphore_wait(barrier, len(partners))

    sent = []

    def remote(src, dst, mask):
        slot = len(sent)
        copy = pltpu.make_async_remote_copy(
            src_ref=src,
            dst_ref=dst,
            send_sem=send_sem.at[slot],
            recv_sem=recv_sem.at[slot],
            device_id=partners[mask],
            device_id_type=MESH,
        )
        copy.start()
        sent.append(copy)
        return copy

    block_rows = coupling.shape[0] // 2
    gram_rows = rank // 2
    my_block = pl.ds(pl.multiple_of(side * block_rows, block_rows), block_rows)
    my_gram = pl.ds(pl.multiple_of(side * gram_rows, gram_rows), gram_rows)
    move = {}
    pending = jnp.int32(0)
    block_of = []

    def send_block(s):
        if s == 0:
            move["block", s] = remote(blocks.at[0], blocks.at[1], 1)
        else:
            place = blocks.at[s + 1, my_block]
            move["block", s] = remote(blocks.at[pending, my_block], place, 1 << s)

    def send_gram(s):
        if s == 0:
            if levels > 1:
                move["rest", s] = remote(gram_local.at[1 - side], gram_in[0], 1)
            move["gram", s] = remote(gram[0].at[0], gram[0].at[1], 1)
            return
        if s + 1 < levels:
            move["rest", s] = remote(gram_rest[s], gram_in[s], 1 << s)
        mine = gram[s].at[0, my_gram]
        move["gram", s] = remote(mine, gram[s].at[1, my_gram], 1 << s)
        move["own", s] = remote(mine, mine, 1)

    def advance_block(s):
        nonlocal pending
        move["block", s].wait_recv()
        block_of.append(jnp.where(bits[s] == 1, pending, s + 1))
        pending = jnp.where(bits[s] == 1, s + 1, pending)
        if s + 1 < levels:
            send_block(s + 1)
        if s > 0:
            block = blocks.at[s + 1, my_block]
            move["block2", s] = remote(block, block, 1)

    def advance_gram(s):
        if s + 1 >= levels:
            return
        move["rest", s].wait_recv()
        here = gram_local[side] if s == 0 else gram_rest[s][...]
        total = (here.astype(F32) + gram_in[s][...].astype(F32)).astype(BF)
        skip = rows[s + 2]
        if s + 2 < levels:
            gram_rest[s + 1][...] = total[:, skip:]
        gram[s + 1][0, my_gram, :] = total[:, :skip]
        send_gram(s + 1)

    def share_gram(s):
        move["gram", s].wait_recv()
        if s > 0:
            other = gram[s].at[1, my_gram]
            move["other", s] = remote(other, other, 1)

    def ready(s):
        if s > 0:
            move["block2", s].wait_recv()
            move["own", s].wait_recv()
            move["other", s].wait_recv()

    c_block.wait()
    send_block(0)

    c_correct.wait()
    c_project.wait()
    c_trend.wait()
    c_inv = local(inverse, inv_v, 5)
    c_obs = local(observed, obs_v, 6)
    c_last = local(trend_correct, trend_v, 7)
    at = 0
    for s in range(0, levels, 2):
        both = min(2, levels - s)
        columns_t = correct_v[:, s * rank : (s + both) * rank].T
        pair = dot(columns_t, basis_v[:, (s + 1) * rank :]).astype(BF)
        for u in range(both):
            value = pair[u * rank : (u + 1) * rank, u * rank :]
            if s + u == 0:
                gram[0][0] = value
            else:
                gram_local[0, :, at : at + rows[s + u + 1]] = value[:gram_rows]
                gram_local[1, :, at : at + rows[s + u + 1]] = value[gram_rows:]
                at += rows[s + u + 1]
    send_gram(0)
    advance_block(0)

    c_order.wait()
    steps = leaf // tile
    column_v[...] = jnp.broadcast_to(order_v[...].astype(F32), (128, leaf)).T
    blocks_wide = leaf // 128

    def make_hot(t, carry):
        place = pl.ds(pl.multiple_of(t * 128, 128), 128)
        column = column_v[place, :]
        lane = lax.broadcasted_iota(jnp.int32, (128, 128), 1).astype(F32)
        for k in range(blocks_wide):
            hit = column == lane + float(128 * k)
            hot_v[place, k * 128 : (k + 1) * 128] = jnp.where(hit, 1.0, 0.0).astype(BF)
        return carry

    lax.fori_loop(0, blocks_wide, make_hot, 0)
    advance_gram(0)
    c_inv.wait()

    if levels > 1:
        advance_block(1)
    c_obs.wait()
    c_last.wait()

    x_move, early, late_move, core_move = {}, {}, {}, {}
    offsets = [[jnp.int32(g * group)] for g in range(groups)]
    finals = []

    def send_x(g, s):
        x_move[g, s] = remote(x_send[g][s], x_recv[g][s], 1 << s)

    def start_group(g):
        lanes = slice(g * group, (g + 1) * group)

        def make_ordered(t, carry):
            r0 = pl.multiple_of(t * tile, tile)
            value = dot(hot_v[pl.ds(r0, tile), :], obs_bf[:, lanes])
            ordered_v[pl.ds(r0, tile), :] = value.astype(BF)
            return carry

        def make_estimate(t, carry):
            r0 = pl.multiple_of(t * tile, tile)
            value = dot(inv_v[pl.ds(r0, tile), :], ordered_v[...])
            est_v[pl.ds(r0, tile), lanes] = value
            est_t[lanes, pl.ds(r0, tile)] = value.astype(BF).T
            return carry

        obs_bf[:, lanes] = obs_v[:, lanes].astype(BF)
        lax.fori_loop(0, steps, make_ordered, 0)
        lax.fori_loop(0, steps, make_estimate, 0)
        sums[g][0][...] = dot(est_t[lanes, :], basis_v[...])
        if held[0] != part[0]:
            away = pl.ds(pl.multiple_of((1 - side) * part[0], part[0]), part[0])
            x_send[g][0][...] = sums[g][0][away, :].astype(BF)
        else:
            x_send[g][0][...] = sums[g][0][...].astype(BF)
        send_x(g, 0)

    def up(g, s):
        count = part[s]
        halves = held[s] != part[s]
        first_side = bits[s] == 0
        offset = offsets[g][s] + (bits[s] * count if halves else 0)
        offset = pl.multiple_of(offset, count)
        offsets[g].append(offset)
        if not halves:
            own = sums[g][s][...]
        else:
            own = sums[g][s][pl.ds(pl.multiple_of(bits[s] * count, count), count), :]
        x_move[g, s].wait_recv()
        if g == 0:
            ready(s)
        other = x_recv[g][s][...].astype(F32)
        own_head, other_head = own[:, :rank], other[:, :rank]
        one = jnp.where(first_side, own_head, other_head).astype(BF)
        two = jnp.where(first_side, other_head, own_head).astype(BF)
        stacked = jnp.concatenate([one, two], 1)
        factor = dot_nt(stacked, blocks[block_of[s]])
        mine = jnp.where(first_side, factor[:, :rank], factor[:, rank:]).astype(BF)
        theirs = jnp.where(first_side, factor[:, rank:], factor[:, :rank]).astype(BF)
        new = (
            own[:, rank:]
            + other[:, rank:]
            - dot(jnp.concatenate([mine, theirs], 1), gram[s][...].reshape(2 * rank, rows[s + 1]))
        )
        sums[g][s + 1][...] = new
        if s + 1 < levels:
            after = part[s + 1]
            if held[s + 1] != after:
                away = pl.multiple_of((1 - bits[s + 1]) * after, after)
                x_send[g][s + 1][...] = sums[g][s + 1][pl.ds(away, after), :].astype(BF)
            else:
                x_send[g][s + 1][...] = new.astype(BF)
            send_x(g, s + 1)
        factors[pl.ds(offset, count), s * rank : (s + 1) * rank] = mine
        if halves:
            sib[g][s][...] = theirs
        if s + 1 == levels:
            trend_factor = dot_nt(new.astype(BF), blocks[pending]).astype(BF)
            factors[pl.ds(offset, count), wide:] = trend_factor
            place = factors.at[pl.ds(offset, count), pl.ds(late * rank, rows[late])]
            for mask in wide_masks:
                late_move[g, mask] = remote(place, place, mask)
        if halves:
            place = factors.at[pl.ds(offset, count), pl.ds(s * rank, rank)]
            masks = [1] if s == 0 else [m for m in wide_masks if m < 2 << s]
            for mask in masks:
                source = sib[g][s] if mask >> s & 1 else place
                early[g, s, mask] = remote(source, place, mask)

    def core_rows(g):
        return pl.ds(pl.multiple_of(g * group + side * part[0], part[0]), part[0])

    def share_early(g):
        for s in split[1:]:
            for mask in wide_masks:
                if (g, s, mask) in early:
                    early[g, s, mask].wait_recv()
        if late > 1:
            place = factors.at[core_rows(g), pl.ds(rank, (late - 1) * rank)]
            core_move[g, 0] = remote(place, place, 1)

    def share_late(g):
        for mask in wide_masks:
            late_move[g, mask].wait_recv()
        place = factors.at[core_rows(g), pl.ds(late * rank, rows[late])]
        core_move[g, 1] = remote(place, place, 1)

    def end_group(g):
        early[g, 0, 1].wait_recv()
        if late > 1:
            core_move[g, 0].wait_recv()
        core_move[g, 1].wait_recv()
        finish(g)

    def finish(g):
        lanes = slice(g * group, (g + 1) * group)

        def apply(t, carry):
            r0 = pl.multiple_of(t * tile, tile)
            place = pl.ds(r0, tile)
            est_v[place, lanes] = (
                est_v[place, lanes]
                - dot_nt(correct_v[place, :], factors[lanes, :wide])
                - dot_nt(trend_v[place, :], factors[lanes, wide:])
            )
            return carry

        lax.fori_loop(0, steps, apply, 0)
        mine = pl.ds(g * group, group)
        finals.append(local(est_v.at[:, mine], out.at[:, mine], 8 + g))

    last = 3 + levels
    for wave in range(last + groups - 1):
        for g in range(groups):
            step = wave - g
            if step < 0 or step >= last:
                continue
            if step == 0:
                start_group(g)
            elif step <= levels:
                if g == 0 and step == 1:
                    share_gram(0)
                up(g, step - 1)
                if g == 0 and step < levels:
                    if step + 1 < levels:
                        advance_block(step + 1)
                    advance_gram(step)
                    share_gram(step)
                if step == levels:
                    share_early(g)
            elif step == levels + 1:
                share_late(g)
            else:
                end_group(g)

    for copy in sent:
        copy.wait_send()
    for copy in finals:
        copy.wait()


def move_kernel(pieces, source, out, held, in_sem, out_sem):
    step = source.shape[0] // pieces
    places = [pl.ds(i * step, step) for i in range(pieces)]
    arrive = [
        pltpu.make_async_copy(source.at[p], held.at[p], in_sem.at[i]) for i, p in enumerate(places)
    ]
    leave = [pltpu.make_async_copy(held.at[p], out.at[p], out_sem.at[i]) for i, p in enumerate(places)]
    for copy in arrive:
        copy.start()
    for first, second in zip(arrive, leave):
        first.wait()
        second.start()
    for copy in leave:
        copy.wait()


def body(
    bits_inner,
    levels,
    observed,
    leaf_order,
    leaf_inverse,
    project_basis,
    correct_basis,
    coupling,
    trend_basis,
    trend_correct,
):
    leaf, cols = observed.shape
    wide = correct_basis.shape[1]
    rank = wide // levels
    trend_rank = trend_basis.shape[1]
    group = 256 if cols % 256 == 0 else cols
    groups = cols // group
    held, part, rows, width = plan(group, levels, rank, trend_rank)
    tile = 512 if leaf % 512 == 0 else leaf
    vm = pltpu.VMEM
    every = range(levels)
    scratch = [
        vm((leaf, cols), F32),
        vm((leaf, cols), BF),
        vm(leaf_order.shape, jnp.int32),
        vm((leaf, leaf), BF),
        vm((leaf, wide + trend_rank), BF),
        vm((leaf, wide), BF),
        vm((leaf, trend_rank), BF),
        vm((leaf, leaf), BF),
        vm((leaf, 128), F32),
        vm((leaf, group), BF),
        vm((leaf, cols), F32),
        vm((cols, leaf), BF),
        vm((levels + 1,) + coupling.shape, BF),
        vm((cols, wide + trend_rank), BF),
        vm((2, rank // 2, max(width[0] - rows[1], rank)), BF),
    ]
    for _ in range(groups):
        scratch += [vm((held[0], rows[0]), F32)]
        scratch += [vm((part[s], rows[s + 1]), F32) for s in every]
    scratch += [vm((part[s], rows[s]), BF) for s in every] * (2 * groups)
    scratch += [vm((part[s], rank), BF) for s in every] * groups
    scratch += [vm((2, rank, rows[s + 1]), BF) for s in every]
    scratch += [vm((rank // 2, width[s + 1]), BF) for s in range(levels - 1)] * 2
    late = sum(held[s] != part[s] for s in every)
    reach = (1 << late >> 1) - 1
    copies = 6 * levels + groups * (levels + 2 * reach + reach + 3)
    scratch += [
        pltpu.SemaphoreType.DMA((8 + groups,)),
        pltpu.SemaphoreType.DMA((copies,)),
        pltpu.SemaphoreType.DMA((copies,)),
    ]
    swept = pl.pallas_call(
        functools.partial(sweep_kernel, bits_inner, levels, rank, group, tile),
        out_shape=jax.ShapeDtypeStruct((leaf, cols), F32),
        in_specs=[pl.BlockSpec(memory_space=pltpu.HBM)] * 8,
        out_specs=pl.BlockSpec(memory_space=pl.ANY),
        scratch_shapes=scratch,
        compiler_params=pltpu.CompilerParams(
            collective_id=0, has_side_effects=True, vmem_limit_bytes=56 * 1024 * 1024
        ),
        name="tree_sweep",
    )(
        observed,
        leaf_order,
        leaf_inverse,
        project_basis,
        correct_basis,
        coupling,
        trend_basis,
        trend_correct,
    )
    pieces = 8 if leaf % 64 == 0 else 1
    return pl.pallas_call(
        functools.partial(move_kernel, pieces),
        out_shape=jax.ShapeDtypeStruct((leaf, cols), F32),
        in_specs=[pl.BlockSpec(memory_space=pl.ANY)],
        out_specs=pl.BlockSpec(memory_space=pl.ANY),
        scratch_shapes=[
            vm((leaf, cols), F32),
            pltpu.SemaphoreType.DMA((pieces,)),
            pltpu.SemaphoreType.DMA((pieces,)),
        ],
        compiler_params=pltpu.CompilerParams(vmem_limit_bytes=62 * 1024 * 1024),
        name="move_result",
    )(swept)


def solution(mesh):
    bits_inner = mesh.shape["inner"].bit_length() - 1
    bits_outer = mesh.shape["outer"].bit_length() - 1
    rows = P(("outer", "inner"), None)
    return jax.shard_map(
        functools.partial(body, bits_inner, bits_inner + bits_outer),
        mesh=mesh,
        in_specs=(rows,) * 8,
        out_specs=rows,
        check_vma=False,
    )
```
